128 devices in a mesh: shot: 8 (over y_lo, x), space: 16 (over y_hi, z, core).
Axes of the slice: x: 4, y: 4 (y_hi: 2, y_lo: 2; y = y_hi * 2 + y_lo), z: 4, core: 2. Of those that a mesh axis runs over, the one named last changes fastest.
Arguments:
- prior_field: bfloat16 [8, 128, 128, 256], P('shot', 'space'), may hold values from -3 to 3
- current_field: bfloat16 [8, 128, 128, 256], P('shot', 'space'), may hold values from -3 to 3
- model_store: bfloat16 [64, 128, 64, 64], P('shot', 'space'), may hold values from 1.5 to 4.5
- tile_home: int32 [64], replicated, may hold values from 0 to 63, as said below
- aperture: int32 [8, 8], replicated, may hold values from 0 to 63, as said below
- source_cell: int32 [8, 3], P('shot'), may hold values from 0 to 254, as said below
- source_frac: int32 [8, 3], P('shot'), may hold values from 0 to 7
- wavelet: float32 [8, 8], P('shot'), may hold values from -8 to 8
- receiver_cell: int32 [8, 16, 64, 3], P('shot', 'space'), may hold values from 0 to 254, as said below
- receiver_frac: int32 [8, 16, 64, 3], P('shot', 'space'), may hold values from 0 to 7
- receiver_count: int32 [8, 16], P('shot', 'space'), may hold values from 1 to 64, 512 in all within a row
- trace_owner: int32 [8, 16, 64, 1], P('shot', 'space'), may hold values from 0 to 7; in each aligned block of 64 rows (0 to 63, 64 to 127, ..., all dimensions but the last counted through in order) at most 16 rows name the same one
Outputs:
- final_field: float32 [8, 128, 128, 256], P('shot', 'space')
- gathers: float32 [8, 16, 8, 128], P('shot', 'space')
The draws below stay inside these ranges and needn't reach their ends.
Inputs may be any that keep to these rules, and one draw needn't show every extreme that they name: `tile_home`: a permutation; lateral tile g = y * 8 + z sits at row y and column z of the survey grid. The tiles of one aperture are distinct; at most 2 of them have the same tile_home // 8, and some aperture has 2 such tiles. `source_cell`: plane below 127, row below 127, column below 255. `receiver_cell`: plane below 7, row below 127, column below 255. `trace_owner`: among the receivers of one device at most 16 name one shot index.
All inputs are finite; a program needn't handle non-finite values. No bound on the sum of `receiver_count` on one device may be relied on, other than what follows from the above.
Results may differ from the reference program's by a relative error of at most 0.0008.
Values may be sent and summed in bfloat16 or wider, within the bound.
No kernel may reach another device: no remote copies, remote signals or barrier semaphores. Data moves between devices by JAX's collectives and lax.ppermute only.
A program may use at most 64 MiB of HBM per device.

```python
import math
import jax
import jax.numpy as jnp
import numpy as np
from jax import lax

TILE = 64
PLANES = 8
AY = 2
AZ = 4
STEPS = 8
R_DEV = 64
NEED = 8
SY = 128
SZ = 256
DEPTH = 128
LY = 8
LZ = 8
LAT = 64
CAPR = 16
N_SHOT = 8
N_SPACE = 16


def draw_tile_home(key, part):
    tile_ids = jnp.arange(LAT, dtype=jnp.int32)
    grid_rows = tile_ids // LZ
    grid_columns = tile_ids % LZ
    pattern_owner = (grid_columns % AZ + AZ * (grid_rows // 2 % 2)) % N_SHOT
    relabel = jax.random.permutation(jax.random.fold_in(key, 1), N_SHOT).astype(jnp.int32)
    owner_ids = relabel[pattern_owner]
    shuffle = jax.random.permutation(jax.random.fold_in(key, 2), LAT).astype(jnp.int32)
    scores = owner_ids * LAT + shuffle
    ordering = jnp.argsort(scores, stable=True).astype(jnp.int32)
    return jnp.argsort(ordering, stable=True).astype(jnp.int32)


def draw_aperture(key, part):
    first_rows = jax.random.randint(jax.random.fold_in(key, 3), (N_SHOT,), 0, LY - 1).astype(jnp.int32)
    even_row = 2 * jax.random.randint(jax.random.fold_in(key, 4), (), 0, LY // 2).astype(jnp.int32)
    first_rows = first_rows.at[0].set(even_row)
    first_rows = first_rows.at[1].set(LY - 2)
    halves = jax.random.randint(jax.random.fold_in(key, 5), (N_SHOT,), 0, 2).astype(jnp.int32)
    halves = halves.at[1].set(1)
    slot_ids = jnp.arange(NEED, dtype=jnp.int32)
    tile_rows = first_rows[:, None] + slot_ids[None, :] // AZ
    tile_columns = AZ * halves[:, None] + slot_ids[None, :] % AZ
    return (tile_rows * LZ + tile_columns).astype(jnp.int32)


def draw_source_cell(key, part):
    limits = jnp.array([DEPTH - 1, SY - 1, SZ - 1], jnp.int32)
    cells = jax.random.randint(jax.random.fold_in(key, 6), (N_SHOT, 3), 0, limits).astype(jnp.int32)
    cells = cells.at[0, 2].set(SZ - 2)
    cells = cells.at[1, 0].set(DEPTH - 2)
    cells = cells.at[2, 1].set(SY - 2)
    return cells.astype(jnp.int32)


def draw_receiver_cell(key, part):
    limits = jnp.array([PLANES - 1, SY - 1, SZ - 1], jnp.int32)
    return jax.random.randint(jax.random.fold_in(key, 7), (N_SHOT, N_SPACE, R_DEV, 3), 0, limits).astype(jnp.int32)


def with_ends(values, own_key, smallest, top_value):
    index_at = [jax.random.randint(jax.random.fold_in(own_key, axis), (), 0, length) for axis, length in enumerate(values.shape)]
    main_axis = values.shape.index(max(values.shape))
    beside = index_at[:main_axis] + [(index_at[main_axis] + 1) % values.shape[main_axis]] + index_at[main_axis + 1:]
    return values.at[tuple(index_at)].set(smallest).at[tuple(beside)].set(top_value)


def shard_levels(key, extent, shards, low, high):
    def one(axis_at, blocks):
        heights = jax.random.uniform(jax.random.fold_in(jax.random.fold_in(key, 6), axis_at), (blocks,), jnp.float32, low / len(shards), high / len(shards))
        return jnp.repeat(jnp.exp(heights), extent[axis_at] // blocks).reshape((-1,) + (1,) * (len(extent) - axis_at - 1))

    level = one(*shards[0])
    for cut in shards[1:]:
        level = level * one(*cut)
    return level


def split_up(amount, total, reach, slope):
    loads = [(1 << 20) // math.isqrt(standing ** slope) + 1 for standing in range(2, amount + 1)]
    spare, given = total - reach - (amount - 1), [1] * (amount - 1)
    while spare > 0:
        movable = [i for i in range(amount - 1) if given[i] < reach]
        pool, remaining = sum([loads[i] for i in movable]), spare
        for i in movable:
            extra = min(reach - given[i], max(1, remaining * loads[i] // pool), spare)
            given[i] = given[i] + extra
            spare = spare - extra
    return np.array([reach] + given)


def ragged(rng, number_of, total, reach, lean):
    if number_of == 2:
        one = jax.random.randint(rng, (), max(1, total - reach), min(reach, total - 1) + 1)
        return jnp.stack([one, total - one])
    lengths = jnp.asarray(split_up(number_of, total, reach, lean), jnp.int32)
    twos = (number_of - 1) // 2
    source_of, taker = lengths[1:1 + 2 * twos:2], lengths[2:2 + 2 * twos:2]
    slack = jnp.minimum(source_of - 1, reach - taker)
    moved = jax.random.randint(jax.random.fold_in(rng, 1), (twos,), 0, 1 << 20) % (slack + 1)
    lengths = lengths.at[1:1 + 2 * twos:2].set(source_of - moved).at[2:2 + 2 * twos:2].set(taker + moved)
    return lengths[jax.random.permutation(jax.random.fold_in(rng, 2), number_of)]


def routed_block(own_key, own, number, rows, amount, top, bound, skew):
    sequence = jax.random.permutation(own_key, amount)
    packed, usual = load_shares(amount, rows * top, bound, skew, True), load_shares(amount, rows * top, bound, skew, False)
    places = jnp.arange(amount)

    def named(tallies, turn):
        used = int((tallies > 0).sum())
        fixed = max(1, used // 4)
        moved = fixed + (places - fixed + turn * (used - fixed)) % max(1, amount - fixed)
        return jnp.zeros((amount,), jnp.int32).at[sequence[jnp.where(places < fixed, places, moved)]].set(jnp.asarray(tallies, jnp.int32))

    tallies = jnp.where(number % 4 == 0, named(packed, number // 4), named(usual, number - number // 4 - 1))
    mixed = jax.random.permutation(jax.random.fold_in(own, 3), amount)
    giver, sink = mixed[0:amount // 2 * 2:2], mixed[1:amount // 2 * 2:2]
    slack = jnp.minimum(tallies[giver] - 1, bound - tallies[sink]) // 2
    slack = jnp.where((giver == sequence[0]) | (sink == sequence[0]) | (tallies[sink] == 0), 0, jnp.maximum(slack, 0))
    moved = jax.random.randint(jax.random.fold_in(own, 4), (amount // 2,), 0, 1 << 20) % (slack + 1)
    tallies = tallies.at[giver].add(-moved).at[sink].add(moved)
    members = jnp.searchsorted(jnp.cumsum(tallies), jnp.arange(rows * top), side="right").astype(jnp.int32)
    listing = members.reshape(top, rows).T
    listing = listing[jax.random.permutation(jax.random.fold_in(own, 1), rows)]
    turn = jax.random.randint(jax.random.fold_in(own, 2), (rows, 1), 0, top)
    return jnp.take_along_axis(listing, (jnp.arange(top)[None, :] + turn) % top, axis=1)


def load_shares(number_of, total, most, slope, full):
    loads = [(1 << 20) // math.isqrt(rank ** slope) + 1 for rank in range(1, number_of + 1)]
    largest = most if full else min(most, max(-(-total // number_of), total * loads[0] // sum(loads)))
    least = 1 if total - largest >= number_of - 1 else 0
    holding, surplus = [largest] + [least] * (number_of - 1), total - largest - least * (number_of - 1)
    while surplus > 0:
        candidates = [i for i in range(1, number_of) if holding[i] < largest] or [i for i in range(1, number_of) if holding[i] < most]
        mass, budget = sum([loads[i] for i in candidates]), surplus
        for i in candidates:
            extra = min(most - holding[i], max(1, budget * loads[i] // mass), surplus)
            holding[i] = holding[i] + extra
            surplus = surplus - extra
    return np.array(holding)


def noise(own_key, extent, scale, bound, shards=(), kind=jnp.bfloat16):
    entries = jax.random.normal(own_key, extent, jnp.float32) * scale
    if len(shards) > 0:
        entries = shard_levels(own_key, extent, shards, -0.22, 0.18) * entries
    return jnp.clip(entries, min=-bound, max=bound).astype(kind)


def setup_inputs(seed: int = 0) -> dict:
    keys = jax.random.split(jax.random.key(seed), 13)
    prior_field = noise(keys[0], (N_SHOT, DEPTH, SY, SZ), 0.5, 3.0, ((0, 8), (1, 16)))
    current_field = noise(keys[1], (N_SHOT, DEPTH, SY, SZ), 0.5, 3.0, ((0, 8), (1, 16)))
    model_store = jnp.clip(1.5 + 3.0 * jax.random.uniform(keys[2], (LAT, DEPTH, TILE, TILE), jnp.float32) ** shard_levels(keys[2], (LAT, DEPTH, TILE, TILE), ((0, 8), (1, 16)), -0.2, 0.2), 1.5, 4.5).astype(jnp.bfloat16)
    tile_home = draw_tile_home(jax.random.fold_in(keys[12], 71), 0)
    aperture = draw_aperture(jax.random.fold_in(keys[12], 71), 0)
    source_cell = draw_source_cell(jax.random.fold_in(keys[12], 71), 0)
    source_frac = with_ends(jax.random.randint(keys[6], (N_SHOT, 3), 0, 8), jax.random.fold_in(keys[6], 1), 0, 7).astype(jnp.int32)
    wavelet = noise(keys[7], (N_SHOT, STEPS), 2.0, 8.0, ((0, 8),), jnp.float32)
    receiver_cell = draw_receiver_cell(jax.random.fold_in(keys[12], 71), 0)
    receiver_frac = with_ends(jax.random.randint(keys[9], (N_SHOT, N_SPACE, R_DEV, 3), 0, 8), jax.random.fold_in(keys[9], 1), 0, 7).astype(jnp.int32)
    receiver_count = jax.vmap(lambda own: ragged(own, N_SPACE, R_DEV * N_SPACE // 2, R_DEV, 2))(jax.random.split(keys[10], N_SHOT)).reshape((N_SHOT, N_SPACE)).astype(jnp.int32)
    trace_owner_keys = jax.random.split(jax.random.fold_in(keys[11], 1), N_SHOT * N_SPACE * R_DEV // R_DEV)
    trace_owner_turns = jax.random.permutation(jax.random.fold_in(keys[11], 3), N_SHOT * N_SPACE * R_DEV // R_DEV)
    trace_owner = jax.vmap(lambda own, number: routed_block(jax.random.fold_in(keys[11], 2), own, number, R_DEV, N_SHOT, 1, CAPR, 2))(trace_owner_keys, trace_owner_turns).reshape((N_SHOT, N_SPACE, R_DEV, 1))
    return {"prior_field": prior_field, "current_field": current_field, "model_store": model_store, "tile_home": tile_home, "aperture": aperture, "source_cell": source_cell, "source_frac": source_frac, "wavelet": wavelet, "receiver_cell": receiver_cell, "receiver_frac": receiver_frac, "receiver_count": receiver_count, "trace_owner": trace_owner}


stencil_weights = (-205.0 / 72.0, 8.0 / 5.0, -1.0 / 5.0, 8.0 / 315.0, -1.0 / 560.0)
courant_scale = 0.09


def laplace(extended, margin):
    depth_planes = extended.shape[0] - 2 * margin
    row_count = extended.shape[1]
    column_count = extended.shape[2]
    lateral = jnp.pad(extended, ((0, 0), (4, 4), (4, 4)))
    centre = lateral[margin:margin + depth_planes, 4:4 + row_count, 4:4 + column_count]
    summed = (3.0 * stencil_weights[0]) * centre
    for distance in range(1, 5):
        neighbours = lateral[margin + distance:margin + distance + depth_planes, 4:4 + row_count, 4:4 + column_count]
        neighbours = neighbours + lateral[margin - distance:margin - distance + depth_planes, 4:4 + row_count, 4:4 + column_count]
        neighbours = neighbours + lateral[margin:margin + depth_planes, 4 + distance:4 + distance + row_count, 4:4 + column_count]
        neighbours = neighbours + lateral[margin:margin + depth_planes, 4 - distance:4 - distance + row_count, 4:4 + column_count]
        neighbours = neighbours + lateral[margin:margin + depth_planes, 4:4 + row_count, 4 + distance:4 + distance + column_count]
        neighbours = neighbours + lateral[margin:margin + depth_planes, 4:4 + row_count, 4 - distance:4 - distance + column_count]
        summed = summed + stencil_weights[distance] * neighbours
    return summed


def velocity_factor(tiles):
    scaled = tiles.astype(jnp.float32) * courant_scale
    return scaled * scaled


def assemble(tiles, tiles_y, tiles_z):
    plane_count = tiles.shape[1]
    edge_cells = tiles.shape[2]
    blocks = tiles.reshape(tiles_y, tiles_z, plane_count, edge_cells, edge_cells)
    return blocks.transpose(2, 0, 3, 1, 4).reshape(plane_count, tiles_y * edge_cells, tiles_z * edge_cells)


def hat_weights(start, fraction, length, offset):
    positions = jnp.arange(length, dtype=jnp.int32) + offset
    share = fraction.astype(jnp.float32) / 8.0
    return jnp.where(positions == start, 1.0 - share, 0.0) + jnp.where(positions == start + 1, share, 0.0)


def source_pattern(cell, fraction, plane_count, row_count, column_count, offset):
    plane_weight = hat_weights(cell[0], fraction[0], plane_count, offset)
    row_weight = hat_weights(cell[1], fraction[1], row_count, 0)
    column_weight = hat_weights(cell[2], fraction[2], column_count, 0)
    return (plane_weight[:, None, None] * row_weight[None, :, None]) * column_weight[None, None, :]


def sample_field(field, cells, fractions):
    flat_field = field.reshape(-1)
    row_count = field.shape[1]
    column_count = field.shape[2]
    share = fractions.astype(jnp.float32) / 8.0
    result = jnp.zeros((cells.shape[0],), jnp.float32)
    for corner in range(8):
        plane_step = corner // 4
        row_step = (corner // 2) % 2
        column_step = corner % 2
        plane_weight = share[:, 0] if plane_step else 1.0 - share[:, 0]
        row_weight = share[:, 1] if row_step else 1.0 - share[:, 1]
        column_weight = share[:, 2] if column_step else 1.0 - share[:, 2]
        position = ((cells[:, 0] + plane_step) * row_count + cells[:, 1] + row_step) * column_count + cells[:, 2] + column_step
        result = result + (plane_weight * row_weight) * column_weight * flat_field[position]
    return result


def reference(prior_field, current_field, model_store, tile_home, aperture, source_cell, source_frac, wavelet, receiver_cell, receiver_frac, receiver_count, trace_owner):
    plane_offsets = (jnp.arange(N_SPACE, dtype=jnp.int32) * PLANES)[None, :, None, None]
    global_cells = jnp.concatenate([receiver_cell[..., 0:1] + plane_offsets, receiver_cell[..., 1:]], axis=-1)
    global_cells = global_cells.reshape(N_SHOT, N_SPACE * R_DEV, 3)
    flat_fractions = receiver_frac.reshape(N_SHOT, N_SPACE * R_DEV, 3)

    def one_group(inputs):
        prior, current, tile_ids, cell, fraction, pulses, cells, fractions = inputs
        tiles = model_store[tile_home[tile_ids]]
        coefficient = velocity_factor(assemble(tiles, AY, AZ))
        pattern = source_pattern(cell, fraction, DEPTH, SY, SZ, 0)
        previous = prior.astype(jnp.float32)
        field = current.astype(jnp.float32)
        samples = []
        for step_number in range(STEPS):
            padded = jnp.pad(field, ((4, 4), (0, 0), (0, 0)))
            following = 2.0 * field - previous + coefficient * laplace(padded, 4) + pulses[step_number] * pattern
            previous, field = field, following
            samples.append(sample_field(field, cells, fractions))
        return field, jnp.stack(samples)

    final_field, samples = lax.map(one_group, (prior_field, current_field, aperture, source_cell, source_frac, wavelet, global_cells, flat_fractions))
    values = samples.reshape(N_SHOT, STEPS, N_SPACE, R_DEV).transpose(0, 2, 3, 1)
    live = jnp.arange(R_DEV, dtype=jnp.int32)[None, None, :] < receiver_count[:, :, None]
    owner_ids = trace_owner[..., 0]
    chosen = ((owner_ids[..., None] == jnp.arange(N_SHOT, dtype=jnp.int32)) & live[..., None]).astype(jnp.int32)
    before = (jnp.cumsum(chosen, axis=2) - chosen).astype(jnp.int32)
    ranks = jnp.sum(before * chosen, axis=3).astype(jnp.int32)
    columns = jnp.arange(N_SHOT, dtype=jnp.int32)[:, None, None] * CAPR + jnp.minimum(ranks, CAPR - 1)
    band_ids = jnp.broadcast_to(jnp.arange(N_SPACE, dtype=jnp.int32)[None, :, None], owner_ids.shape)
    values = jnp.where(live[..., None], values, 0.0)
    gathers = jnp.zeros((N_SHOT, N_SPACE, STEPS, N_SHOT * CAPR), jnp.float32)
    gathers = gathers.at[owner_ids, band_ids, :, columns].add(values)
    return final_field, gathers
```

```python
import jax
import jax.numpy as jnp
import numpy as np
from jax import lax
from jax.experimental import pallas as pl
from jax.experimental.pallas import tpu as pltpu
from jax.sharding import PartitionSpec as P

STEPS = 8
CAPR = 16
PL = 8
ROWS = 128
COLS = 256
EDGE = 64
SLOTS = 64
SCALE = 5040.0
TAPS = (8064.0, -1008.0, 128.0, -9.0)
CENTRE_COLS = -43008.0
CENTRE_ROWS = -42.0
COURANT = 0.09

VMEM = pl.BlockSpec(memory_space=pltpu.VMEM)
SMEM = pl.BlockSpec(memory_space=pltpu.SMEM)
f32 = jnp.float32
bf16 = jnp.bfloat16


def band_matrix(size, centre):
    gap = np.abs(np.arange(size)[:, None] - np.arange(size)[None, :])
    out = np.where(gap == 0, centre, 0.0)
    for k in range(1, 5):
        out = np.where(gap == k, TAPS[k - 1], out)
    return out


def constants():
    cols = band_matrix(COLS, CENTRE_COLS)
    rows = band_matrix(ROWS, CENTRE_ROWS)
    return (
        jnp.asarray(np.concatenate([cols, cols], 0), bf16),
        jnp.asarray(np.concatenate([rows, rows], 1), bf16),
    )


def call(body, outs, ins, scratch=(), limit=None, cost=None):
    return pl.pallas_call(
        body,
        out_shape=[jax.ShapeDtypeStruct(s, d) for s, d in outs],
        in_specs=ins,
        out_specs=[VMEM] * len(outs),
        scratch_shapes=list(scratch),
        compiler_params=pltpu.CompilerParams(vmem_limit_bytes=limit),
        cost_estimate=pl.CostEstimate(flops=cost[0], bytes_accessed=cost[1], transcendentals=0) if cost else None,
    )


def pack_kernel(home, wanted, store, out):
    me = lax.axis_index("shot")

    def group(s, _):
        def slot(j, count):
            row = home[wanted[s, j]]
            mine = row // 8 == me
            for rank in range(2):

                @pl.when(mine & (count == rank))
                def _():
                    out[s, :, :, rank * EDGE : (rank + 1) * EDGE] = store[row % 8]

            return count + mine.astype(jnp.int32)

        lax.fori_loop(0, 8, slot, jnp.int32(0))
        return 0

    lax.fori_loop(0, 8, group, 0)


def assemble_kernel(home, wanted, arrived, own, send_in, send_x):
    me = lax.axis_index("shot")
    even = lax.rem(lax.axis_index("space"), 2) == 0
    owners = []
    ranks = []
    for j in range(8):
        owners.append(home[wanted[me, j]] // 8)
        rank = jnp.int32(0)
        for i in range(j):
            rank = rank + (owners[i] == owners[j]).astype(jnp.int32)
        ranks.append(rank)
    lane = lax.broadcasted_iota(jnp.int32, (EDGE, 2 * EDGE), 1)
    for a in range(2):
        for half in range(2):
            left, right = a * 4 + half * 2, a * 4 + half * 2 + 1
            swap_left = (ranks[left] == 1).astype(jnp.int32)
            swap_right = (ranks[right] == 0).astype(jnp.int32)

            def plane(p, _, left=left, right=right, a=a, half=half, swap_left=swap_left, swap_right=swap_right):
                x = arrived[owners[left], p].astype(f32)
                y = arrived[owners[right], p].astype(f32)
                x = jnp.where(swap_left == 1, pltpu.roll(x, EDGE, 1), x)
                y = jnp.where(swap_right == 1, pltpu.roll(y, EDGE, 1), y)
                both = jnp.where(lane < EDGE, x, y).astype(bf16)
                own[p, a * EDGE : (a + 1) * EDGE, half * 2 * EDGE : (half + 1) * 2 * EDGE] = both
                return 0

            lax.fori_loop(0, PL, plane, 0)
    first_in = jnp.where(even, 4, 0)
    first_x = jnp.where(even, 0, 4)
    send_in[...] = own[pl.ds(first_in, 4)]
    send_x[...] = own[pl.ds(first_x, 4)]


def lateral(weights, across, src, first, count, dst, dst_first=0):
    def body(i, _):
        u = src[first + i]
        hi = u.astype(bf16)
        lo = (u - hi.astype(f32)).astype(bf16)
        lhs = jnp.concatenate([hi, lo, across[...]], 1)
        rhs = jnp.concatenate([weights[...], hi, lo], 0)
        dst[dst_first + i] = jnp.dot(lhs, rhs, preferred_element_type=f32)
        return 0

    lax.fori_loop(0, count, body, 0)


CH_R = 16
CH_C = 128


def tiles(body):
    def step(t, _):
        r = pl.multiple_of(lax.div(t, COLS // CH_C) * CH_R, CH_R)
        c = pl.multiple_of(lax.rem(t, COLS // CH_C) * CH_C, CH_C)
        body(pl.ds(r, CH_R), pl.ds(c, CH_C))
        return 0

    lax.fori_loop(0, (ROWS // CH_R) * (COLS // CH_C), step, 0)


def depth(us, e):
    acc = None
    for k in range(1, 5):
        term = TAPS[k - 1] * (us[e + k] + us[e - k])
        acc = term if acc is None else acc + term
    return acc


def hat(frac):
    share = frac.astype(f32) * 0.125
    return 1.0 - share, share


def add_source(dst, first_plane, count, cell, frac, pulse):
    lane = lax.broadcasted_iota(jnp.int32, (1, COLS), 1)
    wd, wr, wc = hat(frac[0, 0]), hat(frac[0, 1]), hat(frac[0, 2])
    column = jnp.where(lane == cell[0, 2], wc[0], 0.0) + jnp.where(lane == cell[0, 2] + 1, wc[1], 0.0)
    for dp in range(2):
        at = cell[0, 0] + dp - first_plane

        @pl.when((at >= 0) & (at < count))
        def _():
            for dr in range(2):
                row = pl.ds(cell[0, 1] + dr, 1)
                dst[at, row, :] = dst[at, row, :] + pulse * (wd[dp] * wr[dr] * column)


def sample(src, plane_off, n, cells, fracs, count, spread, place, owner, rows, out):
    def one(r, _):
        wd, wr = hat(fracs[0, 0, r, 0]), hat(fracs[0, 0, r, 1])
        p, y = cells[0, 0, r, 0] + plane_off, cells[0, 0, r, 1]
        acc = None
        for dp in range(2):
            for dr in range(2):
                term = (wd[dp] * wr[dr]) * src[p + dp, pl.ds(y + dr, 1), :]
                acc = term if acc is None else acc + term
        rows[pl.ds(r, 1), :] = acc
        return 0

    lax.fori_loop(0, count[0, 0], one, 0)
    slot = lax.broadcasted_iota(jnp.int32, (SLOTS, 1), 0)
    values = jnp.where(slot < count[0, 0], jnp.sum(rows[...] * spread[...], axis=1, keepdims=True), 0.0)
    placed = values * place[...]
    for q in range(8):
        out[q, n : n + 1, :] = jnp.sum(jnp.where(owner[0, 0] == q, placed, 0.0), axis=0, keepdims=True)


def receiver_kernel(cells, fracs, count, owner, spread, place):
    lane = lax.broadcasted_iota(jnp.int32, (SLOTS, COLS), 1)
    share = fracs[0, 0, :, 2:3].astype(f32) * 0.125
    at = cells[0, 0, :, 2:3]
    spread[...] = jnp.where(lane == at, 1.0 - share, 0.0) + jnp.where(lane == at + 1, share, 0.0)
    me = lax.axis_index("shot")
    slot = lax.broadcasted_iota(jnp.int32, (SLOTS, 1), 0)
    live = slot < count[0, 0]
    group = lax.broadcasted_iota(jnp.int32, (SLOTS, 128), 1)
    chosen = jnp.where((owner[0, 0] == group) & live, 1.0, 0.0)
    earlier = jnp.where(
        lax.broadcasted_iota(jnp.int32, (SLOTS, SLOTS), 1) < lax.broadcasted_iota(jnp.int32, (SLOTS, SLOTS), 0), 1.0, 0.0
    )
    before = jnp.dot(earlier.astype(bf16), chosen.astype(bf16), preferred_element_type=f32)
    rank = jnp.sum(before * chosen, axis=1, keepdims=True).astype(jnp.int32)
    place[...] = jnp.where((group == rank + me * CAPR) & live, 1.0, 0.0)


def open_kernel(weights, across, own, got_in, got_x, total, ext):
    even = lax.rem(lax.axis_index("space"), 2) == 0
    at_in = jnp.where(even, 16, 0)
    at_x = jnp.where(even, 0, 16)
    for p in range(PL):
        ext[8 + p] = own[0, p].astype(f32)
        ext[at_in + p] = got_in[0, p].astype(f32)
        ext[at_x + p] = got_x[0, p].astype(f32)
    lateral(weights, across, ext, 4, 16, total)

    def tile(r, c):
        us = [ext[p, r, c] for p in range(24)]
        for i in range(16):
            total[i, r, c] = total[i, r, c] + depth(us, i + 4)

    tiles(tile)


def finish(weights, across, ext_own, previous, coef, u_in, lat, u_out):
    lateral(weights, across, u_in, 4, PL, lat)

    def tile(r, c):
        us = [u_in[p, r, c] for p in range(16)]
        for i in range(PL):
            u_out[i, r, c] = 2.0 * us[i + 4] - previous(i, r, c) + coef[i + 4, r, c] * (lat[i, r, c] + depth(us, i + 4))

    tiles(tile)


def pack_send(u, send_in, send_x):
    even = lax.rem(lax.axis_index("space"), 2) == 0
    for p in range(PL):
        hi = u[p].astype(bf16)
        send_in[p] = hi
        send_x[p] = hi
    near_in = jnp.where(even, PL - 1, 0)
    near_x = jnp.where(even, 0, PL - 1)
    for ref, near in ((send_in, near_in), (send_x, near_x)):
        edge = u[near]
        ref[PL] = (edge - edge.astype(bf16).astype(f32)).astype(bf16)


def first_kernel(
    weights, across, cell, frac, pulses, cells, fracs, count, owner, spread, place,
    total, cur, pri, pri_in, pri_x, v, v_in, v_x,
    next_ext, last, coef, send_in, send_x, gath, lat, rows,
):
    band = lax.axis_index("space")
    even = lax.rem(band, 2) == 0

    def factor(x):
        scaled = x.astype(f32) * COURANT
        return scaled * scaled * (1.0 / SCALE)

    c_in = jnp.where(even, 12, 0)
    c_x = jnp.where(even, 0, 12)
    half_in = jnp.where(even, 0, 4)
    half_x = jnp.where(even, 4, 0)
    for p in range(PL):
        coef[4 + p] = factor(v[p])
        next_ext[4 + p] = 2.0 * cur[0, p].astype(f32) - pri[0, p].astype(f32) + coef[4 + p] * total[4 + p]
    for p in range(4):
        coef[c_in + p] = factor(v_in[p])
        coef[c_x + p] = factor(v_x[p])
    return even, c_in, c_x, half_in, half_x


def round_kernel(
    first_step, weights, across, cell, frac, pulses, cells, fracs, count, owner, spread, place,
    u, got_in, got_x, prev, coef, gath_in,
    next_ext, last, send_in, send_x, gath, ext, lat, rows,
):
    band = lax.axis_index("space")
    even = lax.rem(band, 2) == 0
    at_in = jnp.where(even, 16, 0)
    at_x = jnp.where(even, 0, 16)
    near_in = jnp.where(even, 16, 7)
    near_x = jnp.where(even, 7, 16)
    gath[...] = gath_in[...]
    for p in range(PL):
        ext[8 + p] = u[p]
        ext[at_in + p] = got_in[p].astype(f32)
        ext[at_x + p] = got_x[p].astype(f32)
    ext[near_in] = ext[near_in] + got_in[PL].astype(f32)
    ext[near_x] = ext[near_x] + got_x[PL].astype(f32)
    lateral(weights, across, ext, 4, 16, lat)

    def tile(r, c):
        us = [ext[p, r, c] for p in range(24)]
        for i in range(16):
            next_ext[i, r, c] = 2.0 * us[i + 4] - prev[i, r, c] + coef[i, r, c] * (lat[i, r, c] + depth(us, i + 4))

    tiles(tile)
    add_source(next_ext, band * PL - 4, 16, cell, frac, pulses[0, first_step])
    second_half(first_step, band, weights, across, cell, frac, pulses, cells, fracs, count, owner, spread, place,
                next_ext, lambda i, r, c: u[i, r, c], coef, lat, last, send_in, send_x, gath, rows)


def second_half(first_step, band, weights, across, cell, frac, pulses, cells, fracs, count, owner, spread, place,
                next_ext, previous, coef, lat, last, send_in, send_x, gath, rows):
    finish(weights, across, None, previous, coef, next_ext, lat, last)
    add_source(last, band * PL, PL, cell, frac, pulses[0, first_step + 1])
    if send_in is not None:
        pack_send(last, send_in, send_x)
    sample(next_ext, 4, first_step, cells, fracs, count, spread, place, owner, rows, gath)
    sample(last, 0, first_step + 1, cells, fracs, count, spread, place, owner, rows, gath)


def first_round_kernel(
    weights, across, cell, frac, pulses, cells, fracs, count, owner, spread, place,
    total, cur, cur_in, cur_x, pri, pri_in, pri_x, v, v_in, v_x,
    next_ext, last, coef, send_in, send_x, gath, lat, rows,
):
    band = lax.axis_index("space")
    even = lax.rem(band, 2) == 0

    def factor(x):
        scaled = x.astype(f32) * COURANT
        return scaled * scaled * (1.0 / SCALE)

    def step(at, now, before, vel):
        c = factor(vel)
        coef[at] = c
        next_ext[at] = 2.0 * now.astype(f32) - before.astype(f32) + c * total[at]

    at_in = jnp.where(even, 12, 0)
    at_x = jnp.where(even, 0, 12)
    half_in = jnp.where(even, 0, 4)
    half_x = jnp.where(even, 4, 0)
    for p in range(PL):
        step(4 + p, cur[0, p], pri[0, p], v[p])
    for p in range(4):
        step(at_in + p, cur_in[0, half_in + p], pri_in[0, half_in + p], v_in[p])
        step(at_x + p, cur_x[0, half_x + p], pri_x[0, half_x + p], v_x[p])
    add_source(next_ext, band * PL - 4, 16, cell, frac, pulses[0, 0])
    second_half(0, band, weights, across, cell, frac, pulses, cells, fracs, count, owner, spread, place,
                next_ext, lambda i, r, c: cur[0, i, r, c].astype(f32), coef, lat, last, send_in, send_x, gath, rows)


def last_round_kernel(first_step, *refs):
    refs = list(refs)
    ins, (last, gath, next_ext, ext, lat, rows) = refs[:-6], refs[-6:]
    round_kernel(first_step, *ins, next_ext, last, None, None, gath, ext, lat, rows)


MIB = 1 << 20


def on_device(
    prior_field, current_field, model_store, tile_home, aperture, source_cell, source_frac,
    wavelet, receiver_cell, receiver_frac, receiver_count, trace_owner,
):
    size = lax.axis_size("space")
    pair_in = [(i, i ^ 1) for i in range(size)]
    pair_x = [(i, i + 1) for i in range(1, size - 1, 2)] + [(i + 1, i) for i in range(1, size - 1, 2)]

    def swap(x):
        return lax.ppermute(x, "space", pair_in), lax.ppermute(x, "space", pair_x)

    weights, across = constants()
    out = call(pack_kernel, [((8, PL, EDGE, 2 * EDGE), bf16)], [SMEM, SMEM, VMEM], limit=8 * MIB)(
        tile_home, aperture, model_store
    )[0]
    arrived = lax.all_to_all(out, "shot", split_axis=0, concat_axis=0, tiled=True)
    cur_in, cur_x = swap(current_field)
    pri_in, pri_x = swap(prior_field)
    spread, place = call(
        receiver_kernel, [((SLOTS, COLS), f32), ((SLOTS, 128), f32)], [VMEM, VMEM, SMEM, VMEM], limit=4 * MIB
    )(receiver_cell, receiver_frac, receiver_count, trace_owner)
    plane = (ROWS, COLS)
    total = call(
        open_kernel, [((16,) + plane, f32)], [VMEM] * 5, [pltpu.VMEM((24,) + plane, f32)], limit=16 * MIB
    )(weights, across, current_field, cur_in, cur_x)[0]
    v, v_send_in, v_send_x = call(
        assemble_kernel, [((PL,) + plane, bf16), ((4,) + plane, bf16), ((4,) + plane, bf16)], [SMEM, SMEM, VMEM], limit=8 * MIB
    )(tile_home, aperture, arrived)
    v_in = lax.ppermute(v_send_in, "space", pair_in)
    v_x = lax.ppermute(v_send_x, "space", pair_x)
    common = (
        weights, across, source_cell, source_frac, wavelet, receiver_cell, receiver_frac, receiver_count, trace_owner,
        spread, place,
    )
    specs = [VMEM, VMEM, SMEM, SMEM, SMEM, SMEM, SMEM, SMEM, VMEM, VMEM, VMEM]
    gath_shape = ((8, STEPS, 128), f32)
    send = ((PL + 1,) + plane, bf16)
    ext16 = ((16,) + plane, f32)
    own8 = ((PL,) + plane, f32)
    rows = pltpu.VMEM((SLOTS, COLS), f32)
    prev, u, coef, send_in, send_x, gath = call(
        first_round_kernel, [ext16, own8, ext16, send, send, gath_shape], specs + [VMEM] * 10,
        [pltpu.VMEM(*own8), rows], limit=24 * MIB,
    )(*common, total, current_field, cur_in, cur_x, prior_field, pri_in, pri_x, v, v_in, v_x)
    for r in range(1, 4):
        got_in = lax.ppermute(send_in, "space", pair_in)
        got_x = lax.ppermute(send_x, "space", pair_x)
        args = (*common, u, got_in, got_x, prev, coef, gath)
        scratch = [pltpu.VMEM((24,) + plane, f32), pltpu.VMEM(*ext16), rows]
        if r < 3:
            prev, u, send_in, send_x, gath = call(
                lambda *refs, r=r: round_kernel(2 * r, *refs), [ext16, own8, send, send, gath_shape],
                specs + [VMEM] * 6, scratch, limit=28 * MIB,
            )(*args)
        else:
            u, gath = call(
                lambda *refs, r=r: last_round_kernel(2 * r, *refs), [own8, gath_shape],
                specs + [VMEM] * 6, [pltpu.VMEM(*ext16)] + scratch, limit=28 * MIB,
            )(*args)
    back = lax.all_to_all(gath, "shot", split_axis=0, concat_axis=0, tiled=True)
    return u[None], jnp.sum(back, axis=0)[None, None]


def solution(mesh):
    placed = (
        P("shot", "space", None, None),
        P("shot", "space", None, None),
        P("shot", "space", None, None),
        P(),
        P(),
        P("shot", None),
        P("shot", None),
        P("shot", None),
        P("shot", "space", None, None),
        P("shot", "space", None, None),
        P("shot", "space"),
        P("shot", "space", None, None),
    )
    return jax.shard_map(
        on_device,
        mesh=mesh,
        in_specs=placed,
        out_specs=(P("shot", "space", None, None), P("shot", "space", None, None)),
        check_vma=False,
    )
```

```python
import jax
import jax.numpy as jnp
import numpy as np
from jax import lax
from jax.experimental import pallas as pl
from jax.experimental.pallas import tpu as pltpu
from jax.sharding import PartitionSpec as P

STEPS = 8
CAPR = 16
PL = 8
ROWS = 128
COLS = 256
EDGE = 64
SLOTS = 64
SCALE = 5040.0
TAPS = (8064.0, -1008.0, 128.0, -9.0)
CENTRE_COLS = -43008.0
CENTRE_ROWS = -42.0
COURANT = 0.09

VMEM = pl.BlockSpec(memory_space=pltpu.VMEM)
SMEM = pl.BlockSpec(memory_space=pltpu.SMEM)
HBM = pl.BlockSpec(memory_space=pltpu.HBM)
f32 = jnp.float32
bf16 = jnp.bfloat16


def band_matrix(size, centre):
    gap = np.abs(np.arange(size)[:, None] - np.arange(size)[None, :])
    out = np.where(gap == 0, centre, 0.0)
    for k in range(1, 5):
        out = np.where(gap == k, TAPS[k - 1], out)
    return out


def constants():
    cols = band_matrix(COLS, CENTRE_COLS)
    rows = band_matrix(ROWS, CENTRE_ROWS)
    return (
        jnp.asarray(np.concatenate([cols, cols], 0), bf16),
        jnp.asarray(np.concatenate([rows, rows], 1), bf16),
    )


def call(body, outs, ins, scratch=(), limit=None, cost=None, alias=None):
    return pl.pallas_call(
        body,
        out_shape=[jax.ShapeDtypeStruct(s, d) for s, d in outs],
        in_specs=ins,
        out_specs=[VMEM] * len(outs),
        scratch_shapes=list(scratch),
        input_output_aliases=alias or {},
        compiler_params=pltpu.CompilerParams(vmem_limit_bytes=limit),
        cost_estimate=pl.CostEstimate(flops=cost[0], bytes_accessed=cost[1], transcendentals=0) if cost else None,
    )


def pack_kernel(home_hbm, wanted_hbm, store_hbm, out, home, wanted, store, sems):
    copies = [
        pltpu.make_async_copy(src, dst, sems.at[i])
        for i, (src, dst) in enumerate(((home_hbm, home), (wanted_hbm, wanted), (store_hbm, store)))
    ]
    for copy in copies:
        copy.start()
    copies[0].wait()
    copies[1].wait()
    me = lax.axis_index("shot")
    chosen = []
    for s in range(8):
        count = jnp.int32(0)
        slots = [jnp.int32(0), jnp.int32(0)]
        for j in range(8):
            row = home[wanted[s, j]]
            mine = lax.shift_right_logical(row, 3) == me
            for rank in range(2):
                slots[rank] = jnp.where(mine & (count == rank), row & 7, slots[rank])
            count = count + mine.astype(jnp.int32)
        chosen.append(slots)
    copies[2].wait()
    for s in range(8):
        for p in range(PL):
            out[s, p] = jnp.concatenate([store[chosen[s][0], p], store[chosen[s][1], p]], 1)


def assemble_kernel(home, wanted, arrived, own, send_in, send_x):
    me = lax.axis_index("shot")
    even = lax.rem(lax.axis_index("space"), 2) == 0
    owners = []
    ranks = []
    for j in range(8):
        owners.append(lax.shift_right_logical(home[wanted[me, j]], 3))
        rank = jnp.int32(0)
        for i in range(j):
            rank = rank + (owners[i] == owners[j]).astype(jnp.int32)
        ranks.append(rank)
    for j in range(0, 8, 2):
        rows = slice(j // 4 * EDGE, (j // 4 + 1) * EDGE)
        lanes = slice(j % 4 * EDGE, (j % 4 + 2) * EDGE)
        for p in range(PL):
            halves = []
            for i in (j, j + 1):
                x = arrived[owners[i], p]
                halves.append(jnp.where(ranks[i] == 0, x[:, :EDGE], x[:, EDGE:]))
            own[p, rows, lanes] = jnp.concatenate(halves, 1)
    send_in[...] = own[pl.ds(jnp.where(even, 4, 0), 4)]
    send_x[...] = own[pl.ds(jnp.where(even, 0, 4), 4)]


CHUNK = 16


def product(weights, across, u):
    hi = u.astype(bf16)
    lo = (u - hi.astype(f32)).astype(bf16)
    return jnp.dot(
        jnp.concatenate([hi, lo, across[...]], 1),
        jnp.concatenate([weights[...], hi, lo], 0),
        preferred_element_type=f32,
    )


def chunks():
    return [slice(r, r + CHUNK) for r in range(0, ROWS, CHUNK)]


def depth(get, e, low, high, r, acc):
    for k in range(1, 5):
        parts = [get(p, r) for p in (e + k, e - k) if low <= p < high]
        if parts:
            acc = acc + TAPS[k - 1] * sum(parts[1:], parts[0])
    return acc


def hat(frac):
    share = frac.astype(f32) * 0.125
    return 1.0 - share, share


def add_source(dst, first_plane, count, cell, frac, pulse):
    lane = lax.broadcasted_iota(jnp.int32, (1, COLS), 1)
    wd, wr, wc = hat(frac[0, 0]), hat(frac[0, 1]), hat(frac[0, 2])
    column = jnp.where(lane == cell[0, 2], wc[0], 0.0) + jnp.where(lane == cell[0, 2] + 1, wc[1], 0.0)
    for dp in range(2):
        at = cell[0, 0] + dp - first_plane

        @pl.when((at >= 0) & (at < count))
        def _():
            for dr in range(2):
                row = pl.ds(cell[0, 1] + dr, 1)
                dst[at, row, :] = dst[at, row, :] + pulse * (wd[dp] * wr[dr] * column)


GROUP = 8


def sample(fields, codes, count, spread, place, owner, rows, out):
    def group(g, _):
        for j in range(GROUP):
            r = g * GROUP + j
            code = codes[r]
            wr = hat(code & 7)
            wd = hat(lax.shift_right_logical(code, 3) & 7)
            y = lax.shift_right_logical(code, 6) & 127
            p = lax.shift_right_logical(code, 13)
            for f, (src, off, _) in enumerate(fields):
                acc = None
                for dp in range(2):
                    for dr in range(2):
                        term = (wd[dp] * wr[dr]) * src[p + off + dp, pl.ds(y + dr, 1), :]
                        acc = term if acc is None else acc + term
                rows[f, pl.ds(r, 1), :] = acc
        return 0

    lax.fori_loop(0, lax.div(count[0, 0] + GROUP - 1, GROUP), group, 0)
    live = lax.broadcasted_iota(jnp.int32, (SLOTS, 1), 0) < count[0, 0]
    for f, (_, _, n) in enumerate(fields):
        values = jnp.where(live, jnp.sum(rows[f] * spread[...], axis=1, keepdims=True), 0.0)
        placed = values * place[...]
        for q in range(8):
            out[q, n : n + 1, :] = jnp.sum(jnp.where(owner[0, 0] == q, placed, 0.0), axis=0, keepdims=True)


def receiver_kernel(cells, fracs, count, owner, spread, place):
    lane = lax.broadcasted_iota(jnp.int32, (SLOTS, COLS), 1)
    share = fracs[0, 0, :, 2:3].astype(f32) * 0.125
    at = cells[0, 0, :, 2:3]
    spread[...] = jnp.where(lane == at, 1.0 - share, 0.0) + jnp.where(lane == at + 1, share, 0.0)
    me = lax.axis_index("shot")
    slot = lax.broadcasted_iota(jnp.int32, (SLOTS, 1), 0)
    live = slot < count[0, 0]
    group = lax.broadcasted_iota(jnp.int32, (SLOTS, 128), 1)
    chosen = jnp.where((owner[0, 0] == group) & live, 1.0, 0.0)
    earlier = jnp.where(
        lax.broadcasted_iota(jnp.int32, (SLOTS, SLOTS), 1) < lax.broadcasted_iota(jnp.int32, (SLOTS, SLOTS), 0), 1.0, 0.0
    )
    before = jnp.dot(earlier.astype(bf16), chosen.astype(bf16), preferred_element_type=f32)
    rank = jnp.sum(before * chosen, axis=1, keepdims=True).astype(jnp.int32)
    place[...] = jnp.where((group == rank + me * CAPR) & live, 1.0, 0.0)


def position(even, first, second):
    return jnp.where(even, second, first), jnp.where(even, first, second)


def open_kernel(weights, across, own, got_in, got_x, total, ext):
    even = lax.rem(lax.axis_index("space"), 2) == 0
    at_in, at_x = position(even, 0, 16)
    for p in range(PL):
        ext[8 + p] = own[0, p].astype(f32)
        ext[at_in + p] = got_in[0, p].astype(f32)
        ext[at_x + p] = got_x[0, p].astype(f32)

    def some(g, _):
        for j in range(8):
            i = g * 8 + j
            m = product(weights, across, ext[i + 4])
            for r in chunks():
                total[i, r] = depth(lambda p, r: ext[i + 4 + p, r], 0, -4, 5, r, m[r])
        return 0

    lax.fori_loop(0, 2, some, 0)


def factor(x):
    scaled = x.astype(f32) * COURANT
    return scaled * scaled * (1.0 / SCALE)


def near_kernel(weights, across, cell, frac, pulses, total, cur, pri, v, coef, next_ext, base):
    band = lax.axis_index("space")
    for p in range(PL):
        for r in chunks():
            c = factor(v[p, r])
            coef[4 + p, r] = c
            next_ext[4 + p, r] = 2.0 * cur[0, p, r].astype(f32) - pri[0, p, r].astype(f32) + c * total[4 + p, r]
    add_source(next_ext.at[pl.ds(4, PL)], band * PL, PL, cell, frac, pulses[0, 0])
    for p in range(PL):
        m = product(weights, across, next_ext[4 + p])
        for r in chunks():
            acc = depth(lambda e, r: next_ext[4 + e, r], p, 0, PL, r, m[r])
            base[p, r] = 2.0 * next_ext[4 + p, r] - cur[0, p, r].astype(f32) + coef[4 + p, r] * acc


def add_far(dst, base, coef, far):
    for p in range(PL):
        for r in chunks():
            acc = None
            for k in range(1, 5):
                for e in (p + k, p - k):
                    if not 0 <= e < PL:
                        term = TAPS[k - 1] * far(e, r)
                        acc = term if acc is None else acc + term
            dst(p, r, base[p, r] + coef[4 + p, r] * acc)


def pack_send(u, send_in, send_x):
    even = lax.rem(lax.axis_index("space"), 2) == 0
    for p in range(PL):
        hi = u[p].astype(bf16)
        send_in[p] = hi
        send_x[p] = hi
    near_in, near_x = position(even, 0, PL - 1)
    for ref, near in ((send_in, near_in), (send_x, near_x)):
        edge = u[near]
        ref[PL] = (edge - edge.astype(bf16).astype(f32)).astype(bf16)


def far_kernel(
    cell, frac, pulses, total, cur_in, cur_x, pri_in, pri_x, v_in, v_x, base, coef_in, next_in,
    coef, next_ext, last, send_in, send_x,
):
    band = lax.axis_index("space")
    even = lax.rem(band, 2) == 0
    at_in, at_x = position(even, 0, 12)
    half_in, half_x = position(even, 4, 0)
    for at, half, vel, now, before in ((at_in, half_in, v_in, cur_in, pri_in), (at_x, half_x, v_x, cur_x, pri_x)):
        for p in range(4):
            for r in chunks():
                c = factor(vel[p, r])
                coef[at + p, r] = c
                next_ext[at + p, r] = (
                    2.0 * now[0, half + p, r].astype(f32) - before[0, half + p, r].astype(f32) + c * total[at + p, r]
                )
    add_source(next_ext.at[pl.ds(0, 4)], band * PL - 4, 4, cell, frac, pulses[0, 0])
    add_source(next_ext.at[pl.ds(12, 4)], band * PL + PL, 4, cell, frac, pulses[0, 0])

    def store(p, r, x):
        last[p, r] = x

    add_far(store, base, coef, lambda e, r: next_ext[4 + e, r])
    add_source(last, band * PL, PL, cell, frac, pulses[0, 1])
    pack_send(last, send_in, send_x)


def during_kernel(first_step, weights, across, codes, count, owner, spread, place, u, prev, coef, *rest):
    part, gath, rows = rest[-3:]
    for p in range(PL):
        m = product(weights, across, u[p])
        for r in chunks():
            acc = depth(lambda e, r: u[e, r], p, 0, PL, r, m[r])
            part[p, r] = 2.0 * u[p, r] - prev[4 + p, r] + coef[4 + p, r] * acc
    sample(((prev, 4, first_step - 2), (u, 0, first_step - 1)), codes, count, spread, place, owner, rows, gath)


def after_kernel(
    first_step, weights, across, cell, frac, pulses, u, got_in, got_x, prev, coef, part,
    next_ext, last, halo,
):
    band = lax.axis_index("space")
    even = lax.rem(band, 2) == 0
    at_in, at_x = position(even, 0, PL)
    near_in, near_x = position(even, PL - 1, PL)
    for p in range(PL):
        halo[at_in + p] = got_in[p].astype(f32)
        halo[at_x + p] = got_x[p].astype(f32)
    halo[near_in] = halo[near_in] + got_in[PL].astype(f32)
    halo[near_x] = halo[near_x] + got_x[PL].astype(f32)

    def now(e, r):
        return halo[e + PL, r] if e < 0 else (u[e, r] if e < PL else halo[e, r])

    for e in (-4, -3, -2, -1, 8, 9, 10, 11):
        i = e + 4
        m = product(weights, across, now(e, slice(0, ROWS)))
        for r in chunks():
            acc = depth(now, e, -8, 16, r, m[r])
            next_ext[i, r] = 2.0 * now(e, r) - prev[i, r] + coef[i, r] * acc

    def store(p, r, x):
        next_ext[4 + p, r] = x

    add_far(store, part, coef, now)
    add_source(next_ext, band * PL - 4, 16, cell, frac, pulses[0, first_step])
    for p in range(PL):
        m = product(weights, across, next_ext[4 + p])
        for r in chunks():
            acc = depth(lambda e, r: next_ext[4 + e, r], p, -4, 12, r, m[r])
            last[p, r] = 2.0 * next_ext[4 + p, r] - u[p, r] + coef[4 + p, r] * acc
    add_source(last, band * PL, PL, cell, frac, pulses[0, first_step + 1])


def middle_kernel(first_step, *refs):
    (next_ext, last, send_in, send_x, halo), ins = refs[-5:], refs[:-5]
    after_kernel(first_step, *ins, next_ext, last, halo)
    pack_send(last, send_in, send_x)


def last_kernel(first_step, codes, count, owner, spread, place, gath_in, *refs):
    (last, gath, next_ext, halo, rows), ins = refs[-5:], refs[:-5]
    after_kernel(first_step, *ins, next_ext, last, halo)
    sample(((next_ext, 4, first_step), (last, 0, first_step + 1)), codes, count, spread, place, owner, rows, gath)


MIB = 1 << 20


def on_device(
    prior_field, current_field, model_store, tile_home, aperture, source_cell, source_frac,
    wavelet, receiver_cell, receiver_frac, receiver_count, trace_owner,
):
    size = lax.axis_size("space")
    pair_in = [(i, i ^ 1) for i in range(size)]
    pair_x = [(i, i + 1) for i in range(1, size - 1, 2)] + [(i + 1, i) for i in range(1, size - 1, 2)]

    def swap(in_chip, across_chips):
        return lax.ppermute(in_chip, "space", pair_in), lax.ppermute(across_chips, "space", pair_x)

    weights, across = constants()
    out = call(
        pack_kernel, [((8, PL, EDGE, 2 * EDGE), bf16)], [HBM] * 3,
        [pltpu.SMEM((64,), jnp.int32), pltpu.SMEM((8, 8), jnp.int32), pltpu.VMEM((8, PL, EDGE, EDGE), bf16),
         pltpu.SemaphoreType.DMA((3,))],
        limit=8 * MIB,
    )(tile_home, aperture, model_store)[0]
    arrived = lax.all_to_all(out, "shot", split_axis=0, concat_axis=0, tiled=True)
    cur_in, cur_x = swap(current_field, current_field)
    pri_in, pri_x = swap(prior_field, prior_field)
    spread, place = call(
        receiver_kernel, [((SLOTS, COLS), f32), ((SLOTS, 128), f32)], [VMEM, VMEM, SMEM, VMEM], limit=4 * MIB
    )(receiver_cell, receiver_frac, receiver_count, trace_owner)
    cells, fracs = receiver_cell[0, 0], receiver_frac[0, 0]
    codes = ((cells[:, 0] * ROWS + cells[:, 1]) * 8 + fracs[:, 0]) * 8 + fracs[:, 1]
    plane = (ROWS, COLS)
    own8 = ((PL,) + plane, f32)
    ext16 = ((16,) + plane, f32)
    send = ((PL + 1,) + plane, bf16)
    gath_shape = ((8, STEPS, 128), f32)
    halo = pltpu.VMEM(*ext16)
    rows = pltpu.VMEM((2, SLOTS, COLS), f32)
    total = call(
        open_kernel, [ext16], [VMEM] * 5, [pltpu.VMEM((24,) + plane, f32)], limit=16 * MIB
    )(weights, across, current_field, cur_in, cur_x)[0]
    v, v_send_in, v_send_x = call(
        assemble_kernel, [((PL,) + plane, bf16), ((4,) + plane, bf16), ((4,) + plane, bf16)], [SMEM, SMEM, VMEM], limit=8 * MIB
    )(tile_home, aperture, arrived)
    v_in, v_x = swap(v_send_in, v_send_x)
    source = (source_cell, source_frac, wavelet)
    receivers = (codes, receiver_count, trace_owner, spread, place)
    receiver_specs = [SMEM, SMEM, VMEM, VMEM, VMEM]
    coef, prev, base = call(
        near_kernel, [ext16, ext16, own8], [VMEM] * 2 + [SMEM] * 3 + [VMEM] * 4, limit=16 * MIB
    )(weights, across, *source, total, current_field, prior_field, v)
    coef, prev, u, send_in, send_x = call(
        far_kernel, [ext16, ext16, own8, send, send], [SMEM] * 3 + [VMEM] * 10, limit=24 * MIB, alias={11: 0, 12: 1}
    )(*source, total, cur_in, cur_x, pri_in, pri_x, v_in, v_x, base, coef, prev)
    gath = None
    for n in (2, 4, 6):
        got_in, got_x = swap(send_in, send_x)
        first = gath is None
        part, gath = call(
            lambda *refs, n=n: during_kernel(n, *refs), [own8, gath_shape],
            [VMEM] * 2 + receiver_specs + [VMEM] * (3 if first else 4), [rows], limit=16 * MIB,
            alias={} if first else {10: 1},
        )(weights, across, *receivers, u, prev, coef, *(() if first else (gath,)))
        common = (weights, across, *source, u, got_in, got_x, prev, coef, part)
        common_specs = [VMEM] * 2 + [SMEM] * 3 + [VMEM] * 6
        if n < 6:
            prev, u, send_in, send_x = call(
                lambda *refs, n=n: middle_kernel(n, *refs), [ext16, own8, send, send], common_specs, [halo], limit=24 * MIB
            )(*common)
        else:
            u, gath = call(
                lambda *refs, n=n: last_kernel(n, *refs), [own8, gath_shape],
                receiver_specs + [VMEM] + common_specs, [halo, halo, rows], limit=24 * MIB, alias={5: 1},
            )(*receivers, gath, *common)
    back = lax.all_to_all(gath, "shot", split_axis=0, concat_axis=0, tiled=True)
    return u[None], jnp.sum(back, axis=0)[None, None]


def solution(mesh):
    placed = (
        P("shot", "space", None, None),
        P("shot", "space", None, None),
        P("shot", "space", None, None),
        P(),
        P(),
        P("shot", None),
        P("shot", None),
        P("shot", None),
        P("shot", "space", None, None),
        P("shot", "space", None, None),
        P("shot", "space"),
        P("shot", "space", None, None),
    )
    return jax.shard_map(
        on_device,
        mesh=mesh,
        in_specs=placed,
        out_specs=(P("shot", "space", None, None), P("shot", "space", None, None)),
        check_vma=False,
    )
```

```python
import jax
import jax.numpy as jnp
import numpy as np
from jax import lax
from jax.experimental import pallas as pl
from jax.experimental.pallas import tpu as pltpu
from jax.sharding import PartitionSpec as P

STEPS = 8
CAPR = 16
PL = 8
ROWS = 128
COLS = 256
EDGE = 64
SLOTS = 64
SCALE = 5040.0
TAPS = (8064.0, -1008.0, 128.0, -9.0)
CENTRE_COLS = -43008.0
CENTRE_ROWS = -42.0
COURANT = 0.09
PACK_LIMIT = 56

VMEM = pl.BlockSpec(memory_space=pltpu.VMEM)
SMEM = pl.BlockSpec(memory_space=pltpu.SMEM)
HBM = pl.BlockSpec(memory_space=pltpu.HBM)
f32 = jnp.float32
bf16 = jnp.bfloat16


def band_matrix(size, centre):
    gap = np.abs(np.arange(size)[:, None] - np.arange(size)[None, :])
    out = np.where(gap == 0, centre, 0.0)
    for k in range(1, 5):
        out = np.where(gap == k, TAPS[k - 1], out)
    return out


def constants():
    cols = band_matrix(COLS, CENTRE_COLS)
    rows = band_matrix(ROWS, CENTRE_ROWS)
    return (
        jnp.asarray(np.concatenate([cols, cols], 0), bf16),
        jnp.asarray(np.concatenate([rows, rows], 1), bf16),
    )


def call(body, outs, ins, scratch=(), limit=None, cost=None, alias=None):
    return pl.pallas_call(
        body,
        out_shape=[jax.ShapeDtypeStruct(s, d) for s, d in outs],
        in_specs=ins,
        out_specs=[VMEM] * len(outs),
        scratch_shapes=list(scratch),
        input_output_aliases=alias or {},
        compiler_params=pltpu.CompilerParams(vmem_limit_bytes=limit),
        cost_estimate=pl.CostEstimate(flops=cost[0], bytes_accessed=cost[1], transcendentals=0) if cost else None,
    )


def is_even():
    return lax.rem(lax.axis_index("space"), 2) == 0


def mirrored4(even, plane):
    return jnp.where(even, plane, 3 - plane)


def mirrored(even, plane):
    return jnp.where(even, plane, PL - 1 - plane)


def pack_kernel(home_hbm, wanted_hbm, store_hbm, out, home, wanted, store, sems):
    copies = [
        pltpu.make_async_copy(src, dst, sems.at[i])
        for i, (src, dst) in enumerate(((home_hbm, home), (wanted_hbm, wanted), (store_hbm, store)))
    ]
    for copy in copies:
        copy.start()
    copies[0].wait()
    copies[1].wait()
    me = lax.axis_index("shot")
    even = is_even()
    chosen = []
    for s in range(8):
        count = jnp.int32(0)
        slots = [jnp.int32(0), jnp.int32(0)]
        for j in range(8):
            row = home[wanted[s, j]]
            mine = lax.shift_right_logical(row, 3) == me
            for rank in range(2):
                slots[rank] = jnp.where(mine & (count == rank), row & 7, slots[rank])
            count = count + mine.astype(jnp.int32)
        chosen.append(slots)
    copies[2].wait()
    for s in range(8):
        for q in range(PL):
            p = mirrored(even, q)
            out[s, q] = jnp.concatenate([store[chosen[s][0], p], store[chosen[s][1], p]], 1)


def swapped(x):
    return jnp.concatenate([x[:, EDGE:], x[:, :EDGE]], 1)


def assemble_kernel(home, wanted, arrived, v_x, v_in):
    left = lax.broadcasted_iota(jnp.int32, (EDGE, 2 * EDGE), 1) < EDGE
    me = lax.axis_index("shot")
    owners = []
    ranks = []
    for j in range(8):
        owners.append(lax.shift_right_logical(home[wanted[me, j]], 3))
        rank = jnp.int32(0)
        for i in range(j):
            rank = rank + (owners[i] == owners[j]).astype(jnp.int32)
        ranks.append(rank)
    for j in range(0, 8, 2):
        rows = slice(j // 4 * EDGE, (j // 4 + 1) * EDGE)
        lanes = slice(j % 4 * EDGE, (j % 4 + 2) * EDGE)
        for q in range(PL):
            x = arrived[owners[j], q]
            y = arrived[owners[j + 1], q]
            x = jnp.where(ranks[j] == 0, x, swapped(x))
            y = jnp.where(ranks[j + 1] == 0, swapped(y), y)
            out = v_x if q < 4 else v_in
            out[q % 4, rows, lanes] = jnp.where(left, x, y)


CHUNK = 16


def product(weights, across, u):
    hi = u.astype(bf16)
    lo = (u - hi.astype(f32)).astype(bf16)
    return jnp.dot(
        jnp.concatenate([hi, lo, across[...]], 1),
        jnp.concatenate([weights[...], hi, lo], 0),
        preferred_element_type=f32,
    )


def chunks():
    return [slice(r, r + CHUNK) for r in range(0, ROWS, CHUNK)]


def depth(get, e, low, high, r, acc):
    for k in range(1, 5):
        parts = [get(p, r) for p in (e + k, e - k) if low <= p < high]
        if parts:
            acc = acc + TAPS[k - 1] * sum(parts[1:], parts[0])
    return acc


def hat(frac):
    share = frac.astype(f32) * 0.125
    return 1.0 - share, share


def add_source(parts, even, cell, frac, pulse):
    lane = lax.broadcasted_iota(jnp.int32, (1, COLS), 1)
    wd, wr, wc = hat(frac[0, 0]), hat(frac[0, 1]), hat(frac[0, 2])
    column = jnp.where(lane == cell[0, 2], wc[0], 0.0) + jnp.where(lane == cell[0, 2] + 1, wc[1], 0.0)
    for dp in range(2):
        plane = mirrored(even, cell[0, 0] + dp - lax.axis_index("space") * PL)
        for ref, first, down in parts:
            at = first - plane if down else plane - first

            @pl.when((at >= 0) & (at < ref.shape[0]))
            def _():
                for dr in range(2):
                    row = pl.ds(cell[0, 1] + dr, 1)
                    ref[at, row, :] = ref[at, row, :] + pulse * (wd[dp] * wr[dr] * column)


GROUP = 8


def sample(fields, codes, count, spread, place, owner, rows, out):
    even = is_even()

    def group(g, _):
        for j in range(GROUP):
            r = g * GROUP + j
            code = codes[r]
            wr = hat(code & 7)
            wd = hat(lax.shift_right_logical(code, 3) & 7)
            y = lax.shift_right_logical(code, 6) & 127
            p = lax.shift_right_logical(code, 13)
            for f, (src, mirror, _) in enumerate(fields):
                acc = None
                for dp in range(2):
                    plane = mirrored(even, p + dp) if mirror else p + dp
                    for dr in range(2):
                        term = (wd[dp] * wr[dr]) * src[plane, pl.ds(y + dr, 1), :]
                        acc = term if acc is None else acc + term
                rows[f, pl.ds(r, 1), :] = acc
        return 0

    lax.fori_loop(0, lax.div(count[0, 0] + GROUP - 1, GROUP), group, 0)
    live = lax.broadcasted_iota(jnp.int32, (SLOTS, 1), 0) < count[0, 0]
    for f, (_, _, n) in enumerate(fields):
        values = jnp.where(live, jnp.sum(rows[f] * spread[...], axis=1, keepdims=True), 0.0)
        placed = values * place[...]
        for q in range(8):
            out[q, n : n + 1, :] = jnp.sum(jnp.where(owner[0, 0] == q, placed, 0.0), axis=0, keepdims=True)


def receiver_kernel(cells, fracs, count, owner, spread, place):
    lane = lax.broadcasted_iota(jnp.int32, (SLOTS, COLS), 1)
    share = fracs[0, 0, :, 2:3].astype(f32) * 0.125
    at = cells[0, 0, :, 2:3]
    spread[...] = jnp.where(lane == at, 1.0 - share, 0.0) + jnp.where(lane == at + 1, share, 0.0)
    me = lax.axis_index("shot")
    slot = lax.broadcasted_iota(jnp.int32, (SLOTS, 1), 0)
    live = slot < count[0, 0]
    group = lax.broadcasted_iota(jnp.int32, (SLOTS, 128), 1)
    chosen = jnp.where((owner[0, 0] == group) & live, 1.0, 0.0)
    earlier = jnp.where(
        lax.broadcasted_iota(jnp.int32, (SLOTS, SLOTS), 1) < lax.broadcasted_iota(jnp.int32, (SLOTS, SLOTS), 0), 1.0, 0.0
    )
    before = jnp.dot(earlier.astype(bf16), chosen.astype(bf16), preferred_element_type=f32)
    rank = jnp.sum(before * chosen, axis=1, keepdims=True).astype(jnp.int32)
    place[...] = jnp.where((group == rank + me * CAPR) & live, 1.0, 0.0)


def factor(x):
    scaled = x.astype(f32) * COURANT
    return scaled * scaled * (1.0 / SCALE)


def near_kernel(
    weights, across, cell, frac, pulses, cur, cur_x, cur_in, pri, pri_x, pri_in, own_v_x, own_v_in, v_in,
    coef, coef_in, own, inner, base, outer_lead, outer_sum, halo_x, halo_in,
):
    even = is_even()
    for j in range(PL):
        halo_in[j] = cur_in[0, mirrored(even, j)].astype(f32)
        halo_x[j] = cur_x[0, mirrored(even, PL - 1 - j)].astype(f32)
        base[j] = cur[0, mirrored(even, j)].astype(f32)

    def now(e, r):
        return halo_x[-1 - e, r] if e < 0 else (base[e, r] if e < PL else halo_in[e - PL, r])

    whole = slice(0, ROWS)
    for e in range(-4, 12):
        m = product(weights, across, now(e, whole))
        j = -1 - e if e < 0 else (e if e < PL else e - PL)
        for r in chunks():
            acc = depth(now, e, -8, 16, r, m[r])
            if e < 0:
                outer_sum[j, r] = acc
                outer_lead[j, r] = 2.0 * now(e, r) - pri_x[mirrored4(even, 3 - j), r].astype(f32)
            elif e < PL:
                c = factor((own_v_x if e < 4 else own_v_in)[e % 4, r])
                coef[e, r] = c
                own[e, r] = 2.0 * now(e, r) - pri[0, mirrored(even, e), r].astype(f32) + c * acc
            else:
                c = factor(v_in[3 - j, r])
                coef_in[j, r] = c
                inner[j, r] = 2.0 * now(e, r) - pri_in[mirrored4(even, j), r].astype(f32) + c * acc
    add_source(((own, 0, False), (inner, PL, False)), even, cell, frac, pulses[0, 0])
    for q in range(PL):
        m = product(weights, across, own[q])
        for r in chunks():
            acc = depth(lambda e, r: own[e, r] if e < PL else inner[e - PL, r], q, 0, 12, r, m[r])
            base[q, r] = 2.0 * own[q, r] - base[q, r] + coef[q, r] * acc


def pack_send(u, send_x, send_in):
    for q in range(PL):
        hi = u[q].astype(bf16)
        send_x[q] = hi
        send_in[q] = hi
    for ref, near in ((send_x, 0), (send_in, PL - 1)):
        edge = u[near]
        ref[PL] = (edge - edge.astype(bf16).astype(f32)).astype(bf16)


def far_kernel(
    cell, frac, pulses, outer_lead, outer_sum, v_x, base, coef,
    coef_x, outer, last, send_x, send_in,
):
    even = is_even()
    for j in range(4):
        for r in chunks():
            c = factor(v_x[j, r])
            coef_x[j, r] = c
            outer[j, r] = outer_lead[j, r] + c * outer_sum[j, r]
    add_source(((outer, -1, True),), even, cell, frac, pulses[0, 0])
    for q in range(PL):
        for r in chunks():
            x = base[q, r]
            if q < 4:
                x = x + coef[q, r] * depth(lambda e, r: outer[-1 - e, r], q, -4, 0, r, 0.0)
            last[q, r] = x
    add_source(((last, 0, False),), even, cell, frac, pulses[0, 1])
    pack_send(last, send_x, send_in)


def during_kernel(
    step, weights, across, cell, frac, pulses, codes, count, owner, spread, place, u, prev, prev_in, coef, coef_in, got_in,
    part, own_hi, inner, base, gath, halo, rows,
):
    even = is_even()
    for j in range(PL):
        x = got_in[PL - 1 - j].astype(f32)
        halo[j] = x + got_in[PL].astype(f32) if j == 0 else x

    def now(e, r):
        return u[e, r] if e < PL else halo[e - PL, r]

    whole = slice(0, ROWS)
    for e in range(12):
        m = product(weights, across, now(e, whole))
        for r in chunks():
            acc = depth(now, e, 0, 16, r, m[r])
            if e < PL:
                x = 2.0 * u[e, r] - prev[e, r] + coef[e, r] * acc
                if e < 4:
                    part[e, r] = x
                else:
                    own_hi[e - 4, r] = x
            else:
                inner[e - PL, r] = 2.0 * now(e, r) - prev_in[e - PL, r] + coef_in[e - PL, r] * acc
    add_source(((own_hi, 4, False), (inner, PL, False)), even, cell, frac, pulses[0, step])
    for q in range(4, PL):
        m = product(weights, across, own_hi[q - 4])
        for r in chunks():
            acc = depth(lambda e, r: own_hi[e - 4, r] if e < PL else inner[e - PL, r], q, 4, 12, r, m[r])
            base[q - 4, r] = 2.0 * own_hi[q - 4, r] - u[q, r] + coef[q, r] * acc
    sample(((prev, True, 0), (u, True, 1)), codes, count, spread, place, owner, rows, gath)


def after_kernel(
    step, weights, across, cell, frac, pulses, u, prev, prev_x, coef, coef_x, got_x, part, own_hi, base,
    own, outer, last, halo, place_of,
):
    even = is_even()
    for j in range(PL):
        x = got_x[j].astype(f32)
        halo[j] = x + got_x[PL].astype(f32) if j == 0 else x

    def now(e, r):
        return halo[-1 - e, r] if e < 0 else u[e, r]

    whole = slice(0, ROWS)
    for e in range(-4, 0):
        j = -1 - e
        m = product(weights, across, halo[j])
        for r in chunks():
            acc = depth(now, e, -8, 8, r, m[r])
            outer[j, r] = 2.0 * halo[j, r] - prev_x[j, r] + coef_x[j, r] * acc
    for q in range(4):
        for r in chunks():
            own[q, r] = part[q, r] + coef[q, r] * depth(now, q, -8, 0, r, 0.0)
            own[q + 4, r] = own_hi[q, r]
    add_source(((outer, -1, True), (own.at[pl.ds(0, 4)], 0, False)), even, cell, frac, pulses[0, step])

    def following(e, r):
        return outer[-1 - e, r] if e < 0 else own[e, r]

    for q in range(4):
        m = product(weights, across, own[q])
        for r in chunks():
            acc = depth(following, q, -4, 8, r, m[r])
            last[place_of(q), r] = 2.0 * own[q, r] - u[q, r] + coef[q, r] * acc
    for q in range(4, PL):
        for r in chunks():
            last[place_of(q), r] = base[q - 4, r] + coef[q, r] * depth(following, q, 0, 4, r, 0.0)


def middle_kernel(step, *refs):
    (own, outer, last, send_x, send_in, halo), ins = refs[-6:], refs[:-6]
    after_kernel(step, *ins, own, outer, last, halo, lambda q: q)
    cell, frac, pulses = ins[2:5]
    add_source(((last, 0, False),), is_even(), cell, frac, pulses[0, step + 1])
    pack_send(last, send_x, send_in)


def last_kernel(step, codes, count, owner, spread, place, gath_a, gath_b, gath_c, *refs):
    (final, gath, own, outer, halo, rows), ins = refs[-6:], refs[:-6]
    even = is_even()
    last = final.at[0]
    after_kernel(step, *ins, own, outer, last, halo, lambda q: mirrored(even, q))
    cell, frac, pulses = ins[2:5]
    add_source(((last, 0, False),), True, cell, frac, pulses[0, step + 1])
    for i, some in enumerate((gath_a, gath_b, gath_c)):
        gath[:, 2 * i : 2 * i + 2, :] = some[...]
    sample(((own, True, step), (last, False, step + 1)), codes, count, spread, place, owner, rows, gath)


MIB = 1 << 20


def on_device(
    prior_field, current_field, model_store, tile_home, aperture, source_cell, source_frac,
    wavelet, receiver_cell, receiver_frac, receiver_count, trace_owner,
):
    size = lax.axis_size("space")
    pair_in = [(i, i ^ 1) for i in range(size)]
    pair_x = [(i, i + 1) for i in range(1, size - 1, 2)] + [(i + 1, i) for i in range(1, size - 1, 2)]

    def swap(across_chips, in_chip):
        return lax.ppermute(across_chips, "space", pair_x), lax.ppermute(in_chip, "space", pair_in)

    weights, across = constants()
    plane = (ROWS, COLS)
    four = ((4,) + plane, f32)
    eight = ((PL,) + plane, f32)
    tile_planes = ((4,) + plane, bf16)
    send = ((PL + 1,) + plane, bf16)
    scratch8 = pltpu.VMEM(*eight)
    rows = pltpu.VMEM((2, SLOTS, COLS), f32)

    out = call(
        pack_kernel, [((8, PL, EDGE, 2 * EDGE), bf16)], [HBM] * 3,
        [pltpu.SMEM((64,), jnp.int32), pltpu.SMEM((8, 8), jnp.int32), pltpu.VMEM((8, PL, EDGE, EDGE), bf16),
         pltpu.SemaphoreType.DMA((3,))],
        limit=PACK_LIMIT * MIB,
    )(tile_home, aperture, model_store)[0]
    arrived = lax.all_to_all(out, "shot", split_axis=0, concat_axis=0, tiled=True)
    cur_x, cur_in = swap(current_field, current_field)
    prior = prior_field[0]
    first = jnp.where(is_even(), 0, 4)
    pri_x, pri_in = swap(
        lax.dynamic_slice_in_dim(prior, first, 4, 0), lax.dynamic_slice_in_dim(prior, 4 - first, 4, 0)
    )
    spread, place = call(
        receiver_kernel, [((SLOTS, COLS), f32), ((SLOTS, 128), f32)], [VMEM, VMEM, SMEM, VMEM], limit=4 * MIB
    )(receiver_cell, receiver_frac, receiver_count, trace_owner)
    cells, fracs = receiver_cell[0, 0], receiver_frac[0, 0]
    codes = ((cells[:, 0] * ROWS + cells[:, 1]) * 8 + fracs[:, 0]) * 8 + fracs[:, 1]
    arrived, spread, place, codes = lax.optimization_barrier((arrived, spread, place, codes))
    own_v_x, own_v_in = call(
        assemble_kernel, [tile_planes, tile_planes], [SMEM, SMEM, VMEM], limit=8 * MIB
    )(tile_home, aperture, arrived)
    v_x, v_in = swap(own_v_x, own_v_in)
    source = (source_cell, source_frac, wavelet)
    source_specs = [SMEM] * 3
    receivers = (codes, receiver_count, trace_owner, spread, place)
    receiver_specs = [SMEM, SMEM, VMEM, VMEM, VMEM]
    coef, coef_in, prev, prev_in, base, lead, total = call(
        near_kernel, [eight, four, eight, four, eight, four, four], [VMEM] * 2 + source_specs + [VMEM] * 9,
        [scratch8, scratch8], limit=16 * MIB,
    )(weights, across, *source, current_field, cur_x, cur_in, prior_field, pri_x, pri_in, own_v_x, own_v_in, v_in)
    coef_x, prev_x, u, send_x, send_in = call(
        far_kernel, [four, four, eight, send, send], source_specs + [VMEM] * 5, limit=16 * MIB
    )(*source, lead, total, v_x, base, coef)
    gaths = []
    for n in (2, 4, 6):
        got_x, got_in = swap(send_x, send_in)
        part, own_hi, inner, base, gath = call(
            lambda *refs, n=n: during_kernel(n, *refs), [four, four, four, four, ((8, 2, 128), f32)],
            [VMEM] * 2 + source_specs + receiver_specs + [VMEM] * 6, [scratch8, rows], limit=16 * MIB,
        )(weights, across, *source, *receivers, u, prev, prev_in, coef, coef_in, got_in)
        gaths.append(gath)
        common = (weights, across, *source, u, prev, prev_x, coef, coef_x, got_x, part, own_hi, base)
        common_specs = [VMEM] * 2 + source_specs + [VMEM] * 9
        if n < 6:
            prev, prev_x, u, send_x, send_in = call(
                lambda *refs, n=n: middle_kernel(n, *refs), [eight, four, eight, send, send], common_specs, [scratch8], limit=16 * MIB
            )(*common)
            prev_in = inner
        else:
            final, gath = call(
                lambda *refs, n=n: last_kernel(n, *refs), [((1, PL) + plane, f32), ((8, STEPS, 128), f32)],
                receiver_specs + [VMEM] * 3 + common_specs, [scratch8, pltpu.VMEM(*four), scratch8, rows], limit=20 * MIB,
            )(*receivers, *gaths, *common)
    back = lax.all_to_all(gath, "shot", split_axis=0, concat_axis=0, tiled=True)
    return final, jnp.sum(back, axis=0)[None, None]


def solution(mesh):
    placed = (
        P("shot", "space", None, None),
        P("shot", "space", None, None),
        P("shot", "space", None, None),
        P(),
        P(),
        P("shot", None),
        P("shot", None),
        P("shot", None),
        P("shot", "space", None, None),
        P("shot", "space", None, None),
        P("shot", "space"),
        P("shot", "space", None, None),
    )
    return jax.shard_map(
        on_device,
        mesh=mesh,
        in_specs=placed,
        out_specs=(P("shot", "space", None, None), P("shot", "space", None, None)),
        check_vma=False,
    )
```

```python
import jax
import jax.numpy as jnp
import numpy as np
from jax import lax
from jax.experimental import pallas as pl
from jax.experimental.pallas import tpu as pltpu
from jax.sharding import PartitionSpec as P

STEPS = 8
CAPR = 16
PL = 8
ROWS = 128
COLS = 256
EDGE = 64
SLOTS = 64
SCALE = 5040.0
TAPS = (8064.0, -1008.0, 128.0, -9.0)
CENTRE_COLS = -43008.0
CENTRE_ROWS = -42.0
COURANT = 0.09
PACK_LIMIT = 56

VMEM = pl.BlockSpec(memory_space=pltpu.VMEM)
SMEM = pl.BlockSpec(memory_space=pltpu.SMEM)
HBM = pl.BlockSpec(memory_space=pltpu.HBM)
ANY = pl.BlockSpec(memory_space=pl.ANY)
f32 = jnp.float32
bf16 = jnp.bfloat16


def band_matrix(size, centre):
    gap = np.abs(np.arange(size)[:, None] - np.arange(size)[None, :])
    out = np.where(gap == 0, centre, 0.0)
    for k in range(1, 5):
        out = np.where(gap == k, TAPS[k - 1], out)
    return out


def constants():
    cols = band_matrix(COLS, CENTRE_COLS)
    rows = band_matrix(ROWS, CENTRE_ROWS)
    return (
        jnp.asarray(np.concatenate([cols, cols], 0), bf16),
        jnp.asarray(np.concatenate([rows, rows], 1), bf16),
    )


def call(body, outs, ins, scratch=(), limit=None, cost=None, alias=None, places=None):
    return pl.pallas_call(
        body,
        out_shape=[jax.ShapeDtypeStruct(s, d) for s, d in outs],
        in_specs=ins,
        out_specs=places or [VMEM] * len(outs),
        scratch_shapes=list(scratch),
        input_output_aliases=alias or {},
        compiler_params=pltpu.CompilerParams(vmem_limit_bytes=limit),
        cost_estimate=pl.CostEstimate(flops=cost[0], bytes_accessed=cost[1], transcendentals=0) if cost else None,
    )


def is_even():
    return lax.rem(lax.axis_index("space"), 2) == 0


def mirrored4(even, plane):
    return jnp.where(even, plane, 3 - plane)


def mirrored(even, plane):
    return jnp.where(even, plane, PL - 1 - plane)


def fetch(pairs, sems):
    copies = [pltpu.make_async_copy(src, dst, sems.at[i]) for i, (src, dst) in enumerate(pairs)]
    for copy in copies:
        copy.start()
    return copies


def wait(copies):
    for copy in copies:
        copy.wait()


def pack_kernel(home_hbm, wanted_hbm, store_hbm, out_hbm, home, wanted, store, out, sems, out_sems):
    copies = fetch(((home_hbm, home), (wanted_hbm, wanted), (store_hbm, store)), sems)
    wait(copies[:2])
    me = lax.axis_index("shot")
    even = is_even()
    chosen = []
    for s in range(8):
        count = jnp.int32(0)
        slots = [jnp.int32(0), jnp.int32(0)]
        for j in range(8):
            row = home[wanted[s, j]]
            mine = lax.shift_right_logical(row, 3) == me
            for rank in range(2):
                slots[rank] = jnp.where(mine & (count == rank), row & 7, slots[rank])
            count = count + mine.astype(jnp.int32)
        chosen.append(slots)
    copies[2].wait()
    back = []
    for s in range(8):
        for q in range(PL):
            p = mirrored(even, q)
            out[s, q] = jnp.concatenate([store[chosen[s][0], p], store[chosen[s][1], p]], 1)
        copy = pltpu.make_async_copy(out.at[s], out_hbm.at[s], out_sems.at[s])
        copy.start()
        back.append(copy)
    wait(back)


def plan_kernel(home, wanted, plan):
    me = lax.axis_index("shot")
    spot = lax.broadcasted_iota(jnp.int32, (1, 128), 1)
    listed = jnp.zeros((1, 128), jnp.int32)
    homes = []
    for j in range(8):
        homes.append(lax.shift_right_logical(home[wanted[me, j]], 3))
        nth = jnp.int32(0)
        for i in range(j):
            nth = nth + (homes[i] == homes[j]).astype(jnp.int32)
        listed = jnp.where(spot == j, homes[j], jnp.where(spot == 8 + j, nth, listed))
    plan[...] = listed


def swapped(x):
    return jnp.concatenate([x[:, EDGE:], x[:, :EDGE]], 1)


def assemble_kernel(plan, arrived, v_x, v_in):
    left = lax.broadcasted_iota(jnp.int32, (EDGE, 2 * EDGE), 1) < EDGE
    owners = [plan[0, j] for j in range(8)]
    ranks = [plan[0, 8 + j] for j in range(8)]
    for j in range(0, 8, 2):
        rows = slice(j // 4 * EDGE, (j // 4 + 1) * EDGE)
        lanes = slice(j % 4 * EDGE, (j % 4 + 2) * EDGE)
        for q in range(PL):
            x = arrived[owners[j], q]
            y = arrived[owners[j + 1], q]
            x = jnp.where(ranks[j] == 0, x, swapped(x))
            y = jnp.where(ranks[j + 1] == 0, swapped(y), y)
            out = v_x if q < 4 else v_in
            out[q % 4, rows, lanes] = jnp.where(left, x, y)


CHUNK = 16


def product(weights, across, u):
    hi = u.astype(bf16)
    lo = (u - hi.astype(f32)).astype(bf16)
    return jnp.dot(
        jnp.concatenate([hi, lo, across[...]], 1),
        jnp.concatenate([weights[...], hi, lo], 0),
        preferred_element_type=f32,
    )


def chunks():
    return [slice(r, r + CHUNK) for r in range(0, ROWS, CHUNK)]


def depth(get, e, low, high, r, acc):
    for k in range(1, 5):
        parts = [get(p, r) for p in (e + k, e - k) if low <= p < high]
        if parts:
            acc = acc + TAPS[k - 1] * sum(parts[1:], parts[0])
    return acc


def hat(frac):
    share = frac.astype(f32) * 0.125
    return 1.0 - share, share


def add_source(parts, even, cell, frac, pulse):
    lane = lax.broadcasted_iota(jnp.int32, (1, COLS), 1)
    wd, wr, wc = hat(frac[0, 0]), hat(frac[0, 1]), hat(frac[0, 2])
    column = jnp.where(lane == cell[0, 2], wc[0], 0.0) + jnp.where(lane == cell[0, 2] + 1, wc[1], 0.0)
    for dp in range(2):
        plane = mirrored(even, cell[0, 0] + dp - lax.axis_index("space") * PL)
        for ref, first, down in parts:
            at = first - plane if down else plane - first

            @pl.when((at >= 0) & (at < ref.shape[0]))
            def _():
                for dr in range(2):
                    row = pl.ds(cell[0, 1] + dr, 1)
                    ref[at, row, :] = ref[at, row, :] + pulse * (wd[dp] * wr[dr] * column)


GROUP = 8


def sample(fields, codes, count, spread, place, owner, rows, out):
    even = is_even()

    def group(g, _):
        for j in range(GROUP):
            r = g * GROUP + j
            code = codes[0, r]
            wr = hat(code & 7)
            wd = hat(lax.shift_right_logical(code, 3) & 7)
            y = lax.shift_right_logical(code, 6) & 127
            p = lax.shift_right_logical(code, 13)
            for f, (src, _) in enumerate(fields):
                acc = None
                for dp in range(2):
                    plane = mirrored(even, p + dp)
                    for dr in range(2):
                        term = (wd[dp] * wr[dr]) * src[plane, pl.ds(y + dr, 1), :]
                        acc = term if acc is None else acc + term
                rows[f, pl.ds(r, 1), :] = acc
        return 0

    lax.fori_loop(0, lax.div(count[0, 0] + GROUP - 1, GROUP), group, 0)
    live = lax.broadcasted_iota(jnp.int32, (SLOTS, 1), 0) < count[0, 0]
    for f, (_, n) in enumerate(fields):
        values = jnp.where(live, jnp.sum(rows[f] * spread[...], axis=1, keepdims=True), 0.0)
        placed = values * place[...]
        for q in range(8):
            out[q, n : n + 1, :] = jnp.sum(jnp.where(owner[...] == q, placed, 0.0), axis=0, keepdims=True)


def column(row):
    same = lax.broadcasted_iota(jnp.int32, (SLOTS, SLOTS), 0) == lax.broadcasted_iota(jnp.int32, (SLOTS, SLOTS), 1)
    return jnp.sum(jnp.where(same, row, 0), axis=1, keepdims=True)


def receiver_kernel(count, cells, fracs, owner, spread, place, owners, codes):
    lane = lax.broadcasted_iota(jnp.int32, (SLOTS, COLS), 1)
    share = column(fracs[2:3, :]).astype(f32) * 0.125
    at = column(cells[2:3, :])
    spread[...] = jnp.where(lane == at, 1.0 - share, 0.0) + jnp.where(lane == at + 1, share, 0.0)
    me = lax.axis_index("shot")
    slot = lax.broadcasted_iota(jnp.int32, (SLOTS, 1), 0)
    live = slot < count[0, 0]
    group = lax.broadcasted_iota(jnp.int32, (SLOTS, 128), 1)
    mine = column(owner[...])
    owners[...] = mine
    chosen = jnp.where((mine == group) & live, 1.0, 0.0)
    earlier = jnp.where(
        lax.broadcasted_iota(jnp.int32, (SLOTS, SLOTS), 1) < lax.broadcasted_iota(jnp.int32, (SLOTS, SLOTS), 0), 1.0, 0.0
    )
    before = jnp.dot(earlier.astype(bf16), chosen.astype(bf16), preferred_element_type=f32)
    rank = jnp.sum(before * chosen, axis=1, keepdims=True).astype(jnp.int32)
    place[...] = jnp.where((group == rank + me * CAPR) & live, 1.0, 0.0)
    codes[...] = ((cells[0:1, :] * ROWS + cells[1:2, :]) * 8 + fracs[0:1, :]) * 8 + fracs[1:2, :]

def open_kernel(weights, across, cur, cur_in, pri, pri_in, sums, lead, sums_in, lead_in, u, halo):
    even = is_even()
    for j in range(PL):
        u[j] = cur[0, mirrored(even, j)].astype(f32)
        halo[j] = cur_in[0, mirrored(even, j)].astype(f32)

    def now(e, r):
        return u[e, r] if e < PL else halo[e - PL, r]

    for e in range(12):
        m = product(weights, across, now(e, slice(0, ROWS)))
        for r in chunks():
            acc = depth(now, e, 0, 16, r, m[r])
            if e < PL:
                sums[e, r] = acc
                lead[e, r] = 2.0 * now(e, r) - pri[0, mirrored(even, e), r].astype(f32)
            else:
                sums_in[e - PL, r] = acc
                lead_in[e - PL, r] = 2.0 * now(e, r) - pri_in[mirrored4(even, e - PL), r].astype(f32)


def factor(x):
    scaled = x.astype(f32) * COURANT
    return scaled * scaled * (1.0 / SCALE)


def near_kernel(
    weights, across, cell_any, frac_any, pulses_any, u, sums, lead, own_v_x, own_v_in,
    coef, part, own_hi, base, cell, frac, pulses, sems,
):
    source = fetch(((cell_any, cell), (frac_any, frac), (pulses_any, pulses)), sems)
    for e in range(PL):
        for r in chunks():
            c = factor((own_v_x if e < 4 else own_v_in)[e % 4, r])
            coef[e, r] = c
            x = lead[e, r] + c * sums[e, r]
            if e < 4:
                part[e, r] = x
            else:
                own_hi[e - 4, r] = x
    wait(source)
    add_source(((own_hi, 4, False),), is_even(), cell, frac, pulses[0, 0])
    half_step(weights, across, own_hi, None, u, coef, base)


def half_step(weights, across, own_hi, inner, u, coef, base):
    for q in range(4, PL):
        m = product(weights, across, own_hi[q - 4])
        for r in chunks():
            acc = depth(lambda e, r: own_hi[e - 4, r] if e < PL else inner[e - PL, r], q, 4, 12 if inner is not None else PL, r, m[r])
            base[q - 4, r] = 2.0 * own_hi[q - 4, r] - u[q, r] + coef[q, r] * acc


def cross_kernel(
    weights, across, cell_any, frac_any, pulses_any, u, got_x, coef, part, own_hi, base_hi,
    own, base, outer_lead, outer_sum, halo, cell, frac, pulses, sems,
):
    source = fetch(((cell_any, cell), (frac_any, frac), (pulses_any, pulses)), sems)
    even = is_even()
    for j in range(PL):
        halo[j] = got_x[mirrored(even, PL - 1 - j)].astype(f32)

    def now(e, r):
        return halo[-1 - e, r] if e < 0 else u[e, r]

    for q in range(4):
        for r in chunks():
            own[q, r] = part[q, r] + coef[q, r] * depth(now, q, -8, 0, r, 0.0)
            own[q + 4, r] = own_hi[q, r]
    for e in range(-4, 0):
        j = -1 - e
        m = product(weights, across, halo[j])
        for r in chunks():
            outer_sum[j, r] = depth(now, e, -8, PL, r, m[r])
            outer_lead[j, r] = 2.0 * halo[j, r] - got_x[PL + mirrored4(even, 3 - j), r].astype(f32)
    wait(source)
    add_source(((own.at[pl.ds(0, 4)], 0, False),), even, cell, frac, pulses[0, 0])

    def following(e, r):
        return own[e, r]

    for q in range(4):
        m = product(weights, across, own[q])
        for r in chunks():
            acc = depth(following, q, 0, PL, r, m[r])
            base[q, r] = 2.0 * own[q, r] - u[q, r] + coef[q, r] * acc
    for q in range(4, PL):
        for r in chunks():
            base[q, r] = base_hi[q - 4, r] + coef[q, r] * depth(following, q, 0, 4, r, 0.0)


def bundle_kernel(cur, pri, both, half, sems):
    first = jnp.where(is_even(), 0, 4)
    wait(
        fetch(
            (
                (cur.at[0], both.at[pl.ds(0, PL)]),
                (pri.at[0, pl.ds(first, 4)], both.at[pl.ds(PL, 4)]),
                (pri.at[0, pl.ds(4 - first, 4)], half),
            ),
            sems,
        )
    )


def send_kernel(near, u, out):
    for q in range(PL):
        out[q] = u[q].astype(bf16)
    edge = u[near]
    out[PL] = (edge - edge.astype(bf16).astype(f32)).astype(bf16)


def far_kernel(
    cell_any, frac_any, pulses_any, lead_x, sums_x, v_x, lead_in, sums_in, v_in, base, coef,
    coef_x, coef_in, outer, inner, last, send_x, cell, frac, pulses, sems,
):
    source = fetch(((cell_any, cell), (frac_any, frac), (pulses_any, pulses)), sems)
    even = is_even()
    for j in range(4):
        for r in chunks():
            c = factor(v_x[j, r])
            coef_x[j, r] = c
            outer[j, r] = lead_x[j, r] + c * sums_x[j, r]
            c = factor(v_in[3 - j, r])
            coef_in[j, r] = c
            inner[j, r] = lead_in[j, r] + c * sums_in[j, r]
    wait(source)
    add_source(((outer, -1, True), (inner, PL, False)), even, cell, frac, pulses[0, 0])
    for q in range(PL):
        for r in chunks():
            if q < 4:
                acc = depth(lambda e, r: outer[-1 - e, r], q, -4, 0, r, 0.0)
            else:
                acc = depth(lambda e, r: inner[e - PL, r], q, PL, 12, r, 0.0)
            last[q, r] = base[q, r] + coef[q, r] * acc
    add_source(((last, 0, False),), even, cell, frac, pulses[0, 1])
    send_kernel(0, last, send_x)


def during_kernel(
    step, weights, across, cell_any, frac_any, pulses_any, codes, count, owner, spread, place, u, prev, prev_in, coef, coef_in, got_in,
    part, own_hi, inner, base, gath, halo, rows, cell, frac, pulses, sems,
):
    source = fetch(((cell_any, cell), (frac_any, frac), (pulses_any, pulses)), sems)
    even = is_even()
    for j in range(PL):
        x = got_in[PL - 1 - j].astype(f32)
        halo[j] = x + got_in[PL].astype(f32) if j == 0 else x

    def now(e, r):
        return u[e, r] if e < PL else halo[e - PL, r]

    whole = slice(0, ROWS)
    for e in range(12):
        m = product(weights, across, now(e, whole))
        for r in chunks():
            acc = depth(now, e, 0, 16, r, m[r])
            if e < PL:
                x = 2.0 * u[e, r] - prev[e, r] + coef[e, r] * acc
                if e < 4:
                    part[e, r] = x
                else:
                    own_hi[e - 4, r] = x
            else:
                inner[e - PL, r] = 2.0 * now(e, r) - prev_in[e - PL, r] + coef_in[e - PL, r] * acc
    wait(source)
    add_source(((own_hi, 4, False), (inner, PL, False)), even, cell, frac, pulses[0, step])
    half_step(weights, across, own_hi, inner, u, coef, base)
    sample(((prev, 0), (u, 1)), codes, count, spread, place, owner, rows, gath)


def after_kernel(
    step, weights, across, source, u, prev, prev_x, coef, coef_x, got_x, part, own_hi, base,
    own, outer, last, halo,
):
    copies, cell, frac, pulses = source
    even = is_even()
    for j in range(PL):
        x = got_x[j].astype(f32)
        halo[j] = x + got_x[PL].astype(f32) if j == 0 else x

    def now(e, r):
        return halo[-1 - e, r] if e < 0 else u[e, r]

    whole = slice(0, ROWS)
    for e in range(-4, 0):
        j = -1 - e
        m = product(weights, across, halo[j])
        for r in chunks():
            acc = depth(now, e, -8, 8, r, m[r])
            outer[j, r] = 2.0 * halo[j, r] - prev_x[j, r] + coef_x[j, r] * acc
    for q in range(4):
        for r in chunks():
            own[q, r] = part[q, r] + coef[q, r] * depth(now, q, -8, 0, r, 0.0)
            own[q + 4, r] = own_hi[q, r]
    wait(copies)
    add_source(((outer, -1, True), (own.at[pl.ds(0, 4)], 0, False)), even, cell, frac, pulses[0, step])

    def following(e, r):
        return outer[-1 - e, r] if e < 0 else own[e, r]

    for q in range(4):
        m = product(weights, across, own[q])
        for r in chunks():
            acc = depth(following, q, -4, 8, r, m[r])
            last[q, r] = 2.0 * own[q, r] - u[q, r] + coef[q, r] * acc
    for q in range(4, PL):
        for r in chunks():
            last[q, r] = base[q - 4, r] + coef[q, r] * depth(following, q, 0, 4, r, 0.0)


def middle_kernel(step, weights, across, cell_any, frac_any, pulses_any, *refs):
    own, outer, last, send_x, halo, cell, frac, pulses, sems = refs[-9:]
    copies = fetch(((cell_any, cell), (frac_any, frac), (pulses_any, pulses)), sems)
    source = (copies, cell, frac, pulses)
    after_kernel(step, weights, across, source, *refs[:-9], own, outer, last, halo)
    add_source(((last, 0, False),), is_even(), cell, frac, pulses[0, step + 1])
    send_kernel(0, last, send_x)


def last_kernel(
    step, codes_any, count_any, owner, spread, place, gath_a, gath_b, gath_c,
    weights, across, cell_any, frac_any, pulses_any, *refs,
):
    final, gath, own, outer, last, halo, rows, cell, frac, pulses, sems, codes, count, more_sems, final_sems = refs[-15:]
    copies = fetch(((cell_any, cell), (frac_any, frac), (pulses_any, pulses)), sems)
    more = fetch(((codes_any, codes), (count_any, count)), more_sems)
    even = is_even()
    source = (copies, cell, frac, pulses)
    after_kernel(step, weights, across, source, *refs[:-15], own, outer, last, halo)
    add_source(((last, 0, False),), even, cell, frac, pulses[0, step + 1])
    back = fetch([(last.at[q], final.at[0, mirrored(even, q)]) for q in range(PL)], final_sems)
    for i, some in enumerate((gath_a, gath_b, gath_c)):
        gath[:, 2 * i : 2 * i + 2, :] = some[...]
    wait(more)
    sample(((own, step), (last, step + 1)), codes, count, spread, place, owner, rows, gath)
    wait(back)


MIB = 1 << 20


def on_device(
    prior_field, current_field, model_store, tile_home, aperture, source_cell, source_frac,
    wavelet, receiver_cell, receiver_frac, receiver_count, trace_owner,
):
    size = lax.axis_size("space")
    pair_in = [(i, i ^ 1) for i in range(size)]
    pair_x = [(i, i + 1) for i in range(1, size - 1, 2)] + [(i + 1, i) for i in range(1, size - 1, 2)]

    def swap(across_chips, in_chip):
        return lax.ppermute(across_chips, "space", pair_x), lax.ppermute(in_chip, "space", pair_in)

    weights, across = constants()
    plane = (ROWS, COLS)
    four = ((4,) + plane, f32)
    eight = ((PL,) + plane, f32)
    tile_planes = ((4,) + plane, bf16)
    send = ((PL + 1,) + plane, bf16)
    scratch8 = pltpu.VMEM(*eight)
    rows = pltpu.VMEM((2, SLOTS, COLS), f32)

    out = call(
        pack_kernel, [((8, PL, EDGE, 2 * EDGE), bf16)], [HBM] * 3,
        [pltpu.SMEM((64,), jnp.int32), pltpu.SMEM((8, 8), jnp.int32), pltpu.VMEM((8, PL, EDGE, EDGE), bf16),
         pltpu.VMEM((8, PL, EDGE, 2 * EDGE), bf16), pltpu.SemaphoreType.DMA((3,)), pltpu.SemaphoreType.DMA((8,))],
        limit=PACK_LIMIT * MIB, places=[HBM],
    )(tile_home, aperture, model_store)[0]
    plan = call(plan_kernel, [((1, 128), jnp.int32)], [SMEM, SMEM], limit=4 * MIB)(tile_home, aperture)[0]
    arrived = lax.all_to_all(out, "shot", split_axis=0, concat_axis=0, tiled=True)
    both, half = call(
        bundle_kernel, [((12,) + plane, bf16), tile_planes], [ANY, ANY], [pltpu.SemaphoreType.DMA((3,))],
        limit=4 * MIB, places=[ANY, ANY],
    )(current_field, prior_field)
    first_x, pri_in = swap(both, half)
    cur_in = lax.ppermute(current_field, "space", pair_in)
    spread, place, owners, codes = call(
        receiver_kernel,
        [((SLOTS, COLS), f32), ((SLOTS, 128), f32), ((SLOTS, 1), jnp.int32), ((1, SLOTS), jnp.int32)],
        [SMEM] + [VMEM] * 3, limit=4 * MIB,
    )(
        receiver_count, jnp.transpose(receiver_cell[0, 0]), jnp.transpose(receiver_frac[0, 0]),
        jnp.transpose(trace_owner[0, 0]),
    )
    sums, lead, sums_in, lead_in, u = call(
        open_kernel, [eight, eight, four, four, eight], [VMEM] * 6, [scratch8], limit=16 * MIB
    )(weights, across, current_field, cur_in, prior_field, pri_in)
    arrived, sums, lead, u = lax.optimization_barrier((arrived, sums, lead, u))
    own_v_x, own_v_in = call(
        assemble_kernel, [tile_planes, tile_planes], [SMEM, VMEM], limit=8 * MIB
    )(plan, arrived)
    v_x = lax.ppermute(own_v_x, "space", pair_x)
    source = (source_cell, source_frac, wavelet)
    source_specs = [ANY] * 3
    source_scratch = [
        pltpu.SMEM((1, 3), jnp.int32), pltpu.SMEM((1, 3), jnp.int32), pltpu.SMEM((1, STEPS), f32), pltpu.SemaphoreType.DMA((3,)),
    ]
    receivers = (codes, receiver_count, owners, spread, place)
    receiver_specs = [SMEM, SMEM, VMEM, VMEM, VMEM]
    coef, part, own_hi, base = call(
        near_kernel, [eight, four, four, four], [VMEM] * 2 + source_specs + [VMEM] * 5,
        source_scratch, limit=16 * MIB,
    )(weights, across, *source, u, sums, lead, own_v_x, own_v_in)
    own_v_in, part = lax.optimization_barrier((own_v_in, part))
    v_in = lax.ppermute(own_v_in, "space", pair_in)
    prev, base, lead, total = call(
        cross_kernel, [eight, eight, four, four], [VMEM] * 2 + source_specs + [VMEM] * 6,
        [scratch8] + source_scratch, limit=16 * MIB,
    )(weights, across, *source, u, first_x, coef, part, own_hi, base)
    coef_x, coef_in, prev_x, prev_in, u, send_x = call(
        far_kernel, [four, four, four, four, eight, send], source_specs + [VMEM] * 8, source_scratch, limit=16 * MIB
    )(*source, lead, total, v_x, lead_in, sums_in, v_in, base, coef)
    gaths = []
    for n in (2, 4, 6):
        send_in = call(lambda *refs: send_kernel(PL - 1, *refs), [send], [VMEM], limit=4 * MIB)(u)[0]
        got_x, got_in = swap(send_x, send_in)
        part, own_hi, inner, base, gath = call(
            lambda *refs, n=n: during_kernel(n, *refs), [four, four, four, four, ((8, 2, 128), f32)],
            [VMEM] * 2 + source_specs + receiver_specs + [VMEM] * 6, [scratch8, rows] + source_scratch, limit=16 * MIB,
        )(weights, across, *source, *receivers, u, prev, prev_in, coef, coef_in, got_in)
        gaths.append(gath)
        common = (weights, across, *source, u, prev, prev_x, coef, coef_x, got_x, part, own_hi, base)
        common_specs = [VMEM] * 2 + source_specs + [VMEM] * 9
        if n < 6:
            prev, prev_x, u, send_x = call(
                lambda *refs, n=n: middle_kernel(n, *refs), [eight, four, eight, send], common_specs, [scratch8] + source_scratch, limit=16 * MIB
            )(*common)
            prev_in = inner
        else:
            final, gath = call(
                lambda *refs, n=n: last_kernel(n, *refs), [((1, PL) + plane, f32), ((8, STEPS, 128), f32)],
                [ANY, ANY] + [VMEM] * 6 + common_specs,
                [scratch8, pltpu.VMEM(*four), scratch8, scratch8, rows] + source_scratch
                + [pltpu.SMEM((1, SLOTS), jnp.int32), pltpu.SMEM((1, 1), jnp.int32), pltpu.SemaphoreType.DMA((2,)),
                   pltpu.SemaphoreType.DMA((PL,))],
                limit=20 * MIB, places=[ANY, VMEM],
            )(*receivers, *gaths, *common)
    back = lax.all_to_all(gath, "shot", split_axis=0, concat_axis=0, tiled=True)
    return final, jnp.sum(back, axis=0)[None, None]


def solution(mesh):
    placed = (
        P("shot", "space", None, None),
        P("shot", "space", None, None),
        P("shot", "space", None, None),
        P(),
        P(),
        P("shot", None),
        P("shot", None),
        P("shot", None),
        P("shot", "space", None, None),
        P("shot", "space", None, None),
        P("shot", "space"),
        P("shot", "space", None, None),
    )
    return jax.shard_map(
        on_device,
        mesh=mesh,
        in_specs=placed,
        out_specs=(P("shot", "space", None, None), P("shot", "space", None, None)),
        check_vma=False,
    )
```

```python
import jax
import jax.numpy as jnp
import numpy as np
from jax import lax
from jax.experimental import pallas as pl
from jax.experimental.pallas import tpu as pltpu
from jax.sharding import PartitionSpec as P

STEPS = 8
CAPR = 16
PL = 8
ROWS = 128
COLS = 256
EDGE = 64
SLOTS = 64
SCALE = 5040.0
TAPS = (8064.0, -1008.0, 128.0, -9.0)
CENTRE_COLS = -43008.0
CENTRE_ROWS = -42.0
COURANT = 0.09
PACK_LIMIT = 56

VMEM = pl.BlockSpec(memory_space=pltpu.VMEM)
SMEM = pl.BlockSpec(memory_space=pltpu.SMEM)
HBM = pl.BlockSpec(memory_space=pltpu.HBM)
ANY = pl.BlockSpec(memory_space=pl.ANY)
f32 = jnp.float32
bf16 = jnp.bfloat16


def band_matrix(size, centre):
    gap = np.abs(np.arange(size)[:, None] - np.arange(size)[None, :])
    out = np.where(gap == 0, centre, 0.0)
    for k in range(1, 5):
        out = np.where(gap == k, TAPS[k - 1], out)
    return out


def constants():
    cols = band_matrix(COLS, CENTRE_COLS)
    rows = band_matrix(ROWS, CENTRE_ROWS)
    return (
        jnp.asarray(np.concatenate([cols, cols], 0), bf16),
        jnp.asarray(np.concatenate([rows, rows], 1), bf16),
    )


def call(body, outs, ins, scratch=(), limit=None, cost=None, alias=None, places=None):
    return pl.pallas_call(
        body,
        out_shape=[jax.ShapeDtypeStruct(s, d) for s, d in outs],
        in_specs=ins,
        out_specs=places or [VMEM] * len(outs),
        scratch_shapes=list(scratch),
        input_output_aliases=alias or {},
        compiler_params=pltpu.CompilerParams(vmem_limit_bytes=limit),
        cost_estimate=pl.CostEstimate(flops=cost[0], bytes_accessed=cost[1], transcendentals=0) if cost else None,
    )


def is_even():
    return lax.rem(lax.axis_index("space"), 2) == 0


def mirrored4(even, plane):
    return jnp.where(even, plane, 3 - plane)


def mirrored(even, plane):
    return jnp.where(even, plane, PL - 1 - plane)


def fetch(pairs, sems):
    copies = [pltpu.make_async_copy(src, dst, sems.at[i]) for i, (src, dst) in enumerate(pairs)]
    for copy in copies:
        copy.start()
    return copies


def wait(copies):
    for copy in copies:
        copy.wait()


def pack_kernel(home_hbm, wanted_hbm, store_hbm, out_hbm, home, wanted, store, out, sems, out_sems):
    copies = fetch(((home_hbm, home), (wanted_hbm, wanted), (store_hbm, store)), sems)
    wait(copies[:2])
    me = lax.axis_index("shot")
    even = is_even()
    chosen = []
    for s in range(8):
        count = jnp.int32(0)
        slots = [jnp.int32(0), jnp.int32(0)]
        for j in range(8):
            row = home[wanted[s, j]]
            mine = lax.shift_right_logical(row, 3) == me
            for rank in range(2):
                slots[rank] = jnp.where(mine & (count == rank), row & 7, slots[rank])
            count = count + mine.astype(jnp.int32)
        chosen.append(slots)
    copies[2].wait()
    back = []
    for s in range(8):
        for q in range(PL):
            p = mirrored(even, q)
            out[s, q] = jnp.concatenate([store[chosen[s][0], p], store[chosen[s][1], p]], 1)
        copy = pltpu.make_async_copy(out.at[s], out_hbm.at[s], out_sems.at[s])
        copy.start()
        back.append(copy)
    wait(back)


def plan_kernel(home, wanted, plan):
    me = lax.axis_index("shot")
    spot = lax.broadcasted_iota(jnp.int32, (1, 128), 1)
    listed = jnp.zeros((1, 128), jnp.int32)
    homes = []
    for j in range(8):
        homes.append(lax.shift_right_logical(home[wanted[me, j]], 3))
        nth = jnp.int32(0)
        for i in range(j):
            nth = nth + (homes[i] == homes[j]).astype(jnp.int32)
        listed = jnp.where(spot == j, homes[j], jnp.where(spot == 8 + j, nth, listed))
    plan[...] = listed


def swapped(x):
    return jnp.concatenate([x[:, EDGE:], x[:, :EDGE]], 1)


def assemble_kernel(plan, arrived, v_x, v_in):
    left = lax.broadcasted_iota(jnp.int32, (EDGE, 2 * EDGE), 1) < EDGE
    owners = [plan[0, j] for j in range(8)]
    ranks = [plan[0, 8 + j] for j in range(8)]
    for j in range(0, 8, 2):
        rows = slice(j // 4 * EDGE, (j // 4 + 1) * EDGE)
        lanes = slice(j % 4 * EDGE, (j % 4 + 2) * EDGE)
        for q in range(PL):
            x = arrived[owners[j], q]
            y = arrived[owners[j + 1], q]
            x = jnp.where(ranks[j] == 0, x, swapped(x))
            y = jnp.where(ranks[j + 1] == 0, swapped(y), y)
            out = v_x if q < 4 else v_in
            out[q % 4, rows, lanes] = jnp.where(left, x, y)


CHUNK = 16


def product(weights, across, u):
    hi = u.astype(bf16)
    lo = (u - hi.astype(f32)).astype(bf16)
    return jnp.dot(
        jnp.concatenate([hi, lo, across[...]], 1),
        jnp.concatenate([weights[...], hi, lo], 0),
        preferred_element_type=f32,
    )


def chunks():
    return [slice(r, r + CHUNK) for r in range(0, ROWS, CHUNK)]


def depth(get, e, low, high, r, acc):
    for k in range(1, 5):
        parts = [get(p, r) for p in (e + k, e - k) if low <= p < high]
        if parts:
            acc = acc + TAPS[k - 1] * sum(parts[1:], parts[0])
    return acc


def hat(frac):
    share = frac.astype(f32) * 0.125
    return 1.0 - share, share


def add_source(parts, even, cell, frac, pulse):
    lane = lax.broadcasted_iota(jnp.int32, (1, COLS), 1)
    wd, wr, wc = hat(frac[0, 0]), hat(frac[0, 1]), hat(frac[0, 2])
    column = jnp.where(lane == cell[0, 2], wc[0], 0.0) + jnp.where(lane == cell[0, 2] + 1, wc[1], 0.0)
    for dp in range(2):
        plane = mirrored(even, cell[0, 0] + dp - lax.axis_index("space") * PL)
        for ref, first, down in parts:
            at = first - plane if down else plane - first

            @pl.when((at >= 0) & (at < ref.shape[0]))
            def _():
                for dr in range(2):
                    row = pl.ds(cell[0, 1] + dr, 1)
                    ref[at, row, :] = ref[at, row, :] + pulse * (wd[dp] * wr[dr] * column)


GROUP = 8


def sample(fields, codes, count, spread, place, owner, rows, out):
    even = is_even()

    def group(g, _):
        for j in range(GROUP):
            r = g * GROUP + j
            code = codes[0, r]
            wr = hat(code & 7)
            wd = hat(lax.shift_right_logical(code, 3) & 7)
            y = lax.shift_right_logical(code, 6) & 127
            p = lax.shift_right_logical(code, 13)
            for f, (src, _) in enumerate(fields):
                acc = None
                for dp in range(2):
                    plane = mirrored(even, p + dp)
                    for dr in range(2):
                        term = (wd[dp] * wr[dr]) * src[plane, pl.ds(y + dr, 1), :]
                        acc = term if acc is None else acc + term
                rows[f, pl.ds(r, 1), :] = acc
        return 0

    lax.fori_loop(0, lax.div(count[0, 0] + GROUP - 1, GROUP), group, 0)
    live = lax.broadcasted_iota(jnp.int32, (SLOTS, 1), 0) < count[0, 0]
    for f, (_, n) in enumerate(fields):
        values = jnp.where(live, jnp.sum(rows[f] * spread[...], axis=1, keepdims=True), 0.0)
        placed = values * place[...]
        for q in range(8):
            out[q, n : n + 1, :] = jnp.sum(jnp.where(owner[...] == q, placed, 0.0), axis=0, keepdims=True)


def column(row):
    same = lax.broadcasted_iota(jnp.int32, (SLOTS, SLOTS), 0) == lax.broadcasted_iota(jnp.int32, (SLOTS, SLOTS), 1)
    return jnp.sum(jnp.where(same, row, 0), axis=1, keepdims=True)


def receiver_kernel(count, cells, fracs, owner, spread, place, owners, codes):
    lane = lax.broadcasted_iota(jnp.int32, (SLOTS, COLS), 1)
    share = column(fracs[2:3, :]).astype(f32) * 0.125
    at = column(cells[2:3, :])
    spread[...] = jnp.where(lane == at, 1.0 - share, 0.0) + jnp.where(lane == at + 1, share, 0.0)
    me = lax.axis_index("shot")
    slot = lax.broadcasted_iota(jnp.int32, (SLOTS, 1), 0)
    live = slot < count[0, 0]
    group = lax.broadcasted_iota(jnp.int32, (SLOTS, 128), 1)
    mine = column(owner[...])
    owners[...] = mine
    chosen = jnp.where((mine == group) & live, 1.0, 0.0)
    earlier = jnp.where(
        lax.broadcasted_iota(jnp.int32, (SLOTS, SLOTS), 1) < lax.broadcasted_iota(jnp.int32, (SLOTS, SLOTS), 0), 1.0, 0.0
    )
    before = jnp.dot(earlier.astype(bf16), chosen.astype(bf16), preferred_element_type=f32)
    rank = jnp.sum(before * chosen, axis=1, keepdims=True).astype(jnp.int32)
    place[...] = jnp.where((group == rank + me * CAPR) & live, 1.0, 0.0)
    codes[...] = ((cells[0:1, :] * ROWS + cells[1:2, :]) * 8 + fracs[0:1, :]) * 8 + fracs[1:2, :]

def open_kernel(weights, across, cur, cur_in, pri, pri_in, sums, lead, sums_in, lead_in, u, halo):
    even = is_even()
    for j in range(PL):
        u[j] = cur[0, mirrored(even, j)].astype(f32)
        halo[j] = cur_in[0, mirrored(even, j)].astype(f32)

    def now(e, r):
        return u[e, r] if e < PL else halo[e - PL, r]

    for e in range(12):
        m = product(weights, across, now(e, slice(0, ROWS)))
        for r in chunks():
            acc = depth(now, e, 0, 16, r, m[r])
            if e < PL:
                sums[e, r] = acc
                lead[e, r] = 2.0 * now(e, r) - pri[0, mirrored(even, e), r].astype(f32)
            else:
                sums_in[e - PL, r] = acc
                lead_in[e - PL, r] = 2.0 * now(e, r) - pri_in[mirrored4(even, e - PL), r].astype(f32)


def factor(x):
    scaled = x.astype(f32) * COURANT
    return scaled * scaled * (1.0 / SCALE)


def near_kernel(
    weights, across, cell_any, frac_any, pulses_any, u, sums, lead, own_v_x, own_v_in,
    coef, part, own_hi, base, cell, frac, pulses, sems,
):
    source = fetch(((cell_any, cell), (frac_any, frac), (pulses_any, pulses)), sems)
    for e in range(PL):
        for r in chunks():
            c = factor((own_v_x if e < 4 else own_v_in)[e % 4, r])
            coef[e, r] = c
            x = lead[e, r] + c * sums[e, r]
            if e < 4:
                part[e, r] = x
            else:
                own_hi[e - 4, r] = x
    wait(source)
    add_source(((own_hi, 4, False),), is_even(), cell, frac, pulses[0, 0])
    half_step(weights, across, own_hi, None, u, coef, base)


def half_step(weights, across, own_hi, inner, u, coef, base):
    for q in range(4, PL):
        m = product(weights, across, own_hi[q - 4])
        for r in chunks():
            acc = depth(lambda e, r: own_hi[e - 4, r] if e < PL else inner[e - PL, r], q, 4, 12 if inner is not None else PL, r, m[r])
            base[q - 4, r] = 2.0 * own_hi[q - 4, r] - u[q, r] + coef[q, r] * acc


def cross_kernel(
    weights, across, cell_any, frac_any, pulses_any, u, got_x, coef, part, own_hi, base_hi,
    own, base, outer_lead, outer_sum, halo, cell, frac, pulses, sems,
):
    source = fetch(((cell_any, cell), (frac_any, frac), (pulses_any, pulses)), sems)
    even = is_even()
    for j in range(PL):
        halo[j] = got_x[mirrored(even, PL - 1 - j)].astype(f32)

    def now(e, r):
        return halo[-1 - e, r] if e < 0 else u[e, r]

    for q in range(4):
        for r in chunks():
            own[q, r] = part[q, r] + coef[q, r] * depth(now, q, -8, 0, r, 0.0)
            own[q + 4, r] = own_hi[q, r]
    for e in range(-4, 0):
        j = -1 - e
        m = product(weights, across, halo[j])
        for r in chunks():
            outer_sum[j, r] = depth(now, e, -8, PL, r, m[r])
            outer_lead[j, r] = 2.0 * halo[j, r] - got_x[PL + mirrored4(even, 3 - j), r].astype(f32)
    wait(source)
    add_source(((own.at[pl.ds(0, 4)], 0, False),), even, cell, frac, pulses[0, 0])

    def following(e, r):
        return own[e, r]

    for q in range(4):
        m = product(weights, across, own[q])
        for r in chunks():
            acc = depth(following, q, 0, PL, r, m[r])
            base[q, r] = 2.0 * own[q, r] - u[q, r] + coef[q, r] * acc
    for q in range(4, PL):
        for r in chunks():
            base[q, r] = base_hi[q - 4, r] + coef[q, r] * depth(following, q, 0, 4, r, 0.0)


def bundle_kernel(cur, pri, both, half, sems):
    first = jnp.where(is_even(), 0, 4)
    wait(
        fetch(
            (
                (cur.at[0], both.at[pl.ds(0, PL)]),
                (pri.at[0, pl.ds(first, 4)], both.at[pl.ds(PL, 4)]),
                (pri.at[0, pl.ds(4 - first, 4)], half),
            ),
            sems,
        )
    )


def pack_send(u, out):
    for q in range(PL):
        out[q] = u[q].astype(bf16)
    if out.shape[0] > PL:
        edge = u[0]
        out[PL] = (edge - edge.astype(bf16).astype(f32)).astype(bf16)


def far_kernel(
    cell, frac, pulses, lead_x, sums_x, v_x, lead_in, sums_in, v_in, base, coef,
    coef_x, coef_in, outer, inner, last, send_x,
):
    even = is_even()
    for j in range(4):
        for r in chunks():
            c = factor(v_x[j, r])
            coef_x[j, r] = c
            outer[j, r] = lead_x[j, r] + c * sums_x[j, r]
            c = factor(v_in[3 - j, r])
            coef_in[j, r] = c
            inner[j, r] = lead_in[j, r] + c * sums_in[j, r]
    add_source(((outer, -1, True), (inner, PL, False)), even, cell, frac, pulses[0, 0])
    for q in range(PL):
        for r in chunks():
            if q < 4:
                acc = depth(lambda e, r: outer[-1 - e, r], q, -4, 0, r, 0.0)
            else:
                acc = depth(lambda e, r: inner[e - PL, r], q, PL, 12, r, 0.0)
            last[q, r] = base[q, r] + coef[q, r] * acc
    add_source(((last, 0, False),), even, cell, frac, pulses[0, 1])
    pack_send(last, send_x)


def during_kernel(
    step, weights, across, cell_any, frac_any, pulses_any, codes, count, owner, spread, place, u, prev, prev_in, coef, coef_in, got_in,
    part, own_hi, inner, base, gath, rows, cell, frac, pulses, sems,
):
    source = fetch(((cell_any, cell), (frac_any, frac), (pulses_any, pulses)), sems)
    even = is_even()
    def now(e, r):
        return u[e, r] if e < PL else got_in[2 * PL - 1 - e, r]

    whole = slice(0, ROWS)
    for e in range(12):
        m = product(weights, across, now(e, whole))
        for r in chunks():
            acc = depth(now, e, 0, 16, r, m[r])
            if e < PL:
                x = 2.0 * u[e, r] - prev[e, r] + coef[e, r] * acc
                if e < 4:
                    part[e, r] = x
                else:
                    own_hi[e - 4, r] = x
            else:
                inner[e - PL, r] = 2.0 * now(e, r) - prev_in[e - PL, r] + coef_in[e - PL, r] * acc
    wait(source)
    add_source(((own_hi, 4, False), (inner, PL, False)), even, cell, frac, pulses[0, step])
    half_step(weights, across, own_hi, inner, u, coef, base)
    sample(((prev, 0), (u, 1)), codes, count, spread, place, owner, rows, gath)


def after_kernel(
    step, weights, across, source, u, prev, prev_x, coef, coef_x, got_x, part, own_hi, base,
    own, outer, last, halo,
):
    copies, cell, frac, pulses = source
    even = is_even()
    for j in range(PL):
        x = got_x[j].astype(f32)
        halo[j] = x + got_x[PL].astype(f32) if j == 0 and got_x.shape[0] > PL else x

    def now(e, r):
        return halo[-1 - e, r] if e < 0 else u[e, r]

    whole = slice(0, ROWS)
    for e in range(-4, 0):
        j = -1 - e
        m = product(weights, across, halo[j])
        for r in chunks():
            acc = depth(now, e, -8, 8, r, m[r])
            outer[j, r] = 2.0 * halo[j, r] - prev_x[j, r] + coef_x[j, r] * acc
    for q in range(4):
        for r in chunks():
            own[q, r] = part[q, r] + coef[q, r] * depth(now, q, -8, 0, r, 0.0)
            own[q + 4, r] = own_hi[q, r]
    wait(copies)
    add_source(((outer, -1, True), (own.at[pl.ds(0, 4)], 0, False)), even, cell, frac, pulses[0, step])

    def following(e, r):
        return outer[-1 - e, r] if e < 0 else own[e, r]

    for q in range(4):
        m = product(weights, across, own[q])
        for r in chunks():
            acc = depth(following, q, -4, 8, r, m[r])
            last[q, r] = 2.0 * own[q, r] - u[q, r] + coef[q, r] * acc
    for q in range(4, PL):
        for r in chunks():
            last[q, r] = base[q - 4, r] + coef[q, r] * depth(following, q, 0, 4, r, 0.0)


def middle_kernel(step, weights, across, cell_any, frac_any, pulses_any, *refs):
    own, outer, last, send_x, halo, cell, frac, pulses, sems = refs[-9:]
    copies = fetch(((cell_any, cell), (frac_any, frac), (pulses_any, pulses)), sems)
    source = (copies, cell, frac, pulses)
    after_kernel(step, weights, across, source, *refs[:-9], own, outer, last, halo)
    add_source(((last, 0, False),), is_even(), cell, frac, pulses[0, step + 1])
    pack_send(last, send_x)


def last_kernel(
    step, codes_any, count_any, owner, spread, place, gath_a, gath_b, gath_c,
    weights, across, cell_any, frac_any, pulses_any, *refs,
):
    final, gath, own, outer, last, halo, rows, cell, frac, pulses, sems, codes, count, more_sems, final_sems = refs[-15:]
    copies = fetch(((cell_any, cell), (frac_any, frac), (pulses_any, pulses)), sems)
    more = fetch(((codes_any, codes), (count_any, count)), more_sems)
    even = is_even()
    source = (copies, cell, frac, pulses)
    after_kernel(step, weights, across, source, *refs[:-15], own, outer, last, halo)
    add_source(((last, 0, False),), even, cell, frac, pulses[0, step + 1])
    back = fetch([(last.at[q], final.at[0, mirrored(even, q)]) for q in range(PL)], final_sems)
    for i, some in enumerate((gath_a, gath_b, gath_c)):
        gath[:, 2 * i : 2 * i + 2, :] = some[...]
    wait(more)
    sample(((own, step), (last, step + 1)), codes, count, spread, place, owner, rows, gath)
    wait(back)


MIB = 1 << 20


def on_device(
    prior_field, current_field, model_store, tile_home, aperture, source_cell, source_frac,
    wavelet, receiver_cell, receiver_frac, receiver_count, trace_owner,
):
    size = lax.axis_size("space")
    pair_in = [(i, i ^ 1) for i in range(size)]
    pair_x = [(i, i + 1) for i in range(1, size - 1, 2)] + [(i + 1, i) for i in range(1, size - 1, 2)]

    def swap(across_chips, in_chip):
        return lax.ppermute(across_chips, "space", pair_x), lax.ppermute(in_chip, "space", pair_in)

    weights, across = constants()
    plane = (ROWS, COLS)
    four = ((4,) + plane, f32)
    eight = ((PL,) + plane, f32)
    tile_planes = ((4,) + plane, bf16)
    send = ((PL + 1,) + plane, bf16)
    scratch8 = pltpu.VMEM(*eight)
    rows = pltpu.VMEM((2, SLOTS, COLS), f32)

    out = call(
        pack_kernel, [((8, PL, EDGE, 2 * EDGE), bf16)], [HBM] * 3,
        [pltpu.SMEM((64,), jnp.int32), pltpu.SMEM((8, 8), jnp.int32), pltpu.VMEM((8, PL, EDGE, EDGE), bf16),
         pltpu.VMEM((8, PL, EDGE, 2 * EDGE), bf16), pltpu.SemaphoreType.DMA((3,)), pltpu.SemaphoreType.DMA((8,))],
        limit=PACK_LIMIT * MIB, places=[HBM],
    )(tile_home, aperture, model_store)[0]
    plan = call(plan_kernel, [((1, 128), jnp.int32)], [SMEM, SMEM], limit=4 * MIB)(tile_home, aperture)[0]
    arrived = lax.all_to_all(out, "shot", split_axis=0, concat_axis=0, tiled=True)
    both, half = call(
        bundle_kernel, [((12,) + plane, bf16), tile_planes], [ANY, ANY], [pltpu.SemaphoreType.DMA((3,))],
        limit=4 * MIB, places=[ANY, ANY],
    )(current_field, prior_field)
    first_x, pri_in = swap(both, half)
    cur_in = lax.ppermute(current_field, "space", pair_in)
    spread, place, owners, codes = call(
        receiver_kernel,
        [((SLOTS, COLS), f32), ((SLOTS, 128), f32), ((SLOTS, 1), jnp.int32), ((1, SLOTS), jnp.int32)],
        [SMEM] + [VMEM] * 3, limit=4 * MIB,
    )(
        receiver_count, jnp.transpose(receiver_cell[0, 0]), jnp.transpose(receiver_frac[0, 0]),
        jnp.transpose(trace_owner[0, 0]),
    )
    sums, lead, sums_in, lead_in, u = call(
        open_kernel, [eight, eight, four, four, eight], [VMEM] * 6, [scratch8], limit=16 * MIB
    )(weights, across, current_field, cur_in, prior_field, pri_in)
    arrived, sums, lead, u = lax.optimization_barrier((arrived, sums, lead, u))
    own_v_x, own_v_in = call(
        assemble_kernel, [tile_planes, tile_planes], [VMEM, VMEM], limit=8 * MIB
    )(plan, arrived)
    v_x = lax.ppermute(own_v_x, "space", pair_x)
    source = (source_cell, source_frac, wavelet)
    source_specs = [ANY] * 3
    source_scratch = [
        pltpu.SMEM((1, 3), jnp.int32), pltpu.SMEM((1, 3), jnp.int32), pltpu.SMEM((1, STEPS), f32), pltpu.SemaphoreType.DMA((3,)),
    ]
    receivers = (codes, receiver_count, owners, spread, place)
    receiver_specs = [SMEM, SMEM, VMEM, VMEM, VMEM]
    coef, part, own_hi, base = call(
        near_kernel, [eight, four, four, four], [VMEM] * 2 + source_specs + [VMEM] * 5,
        source_scratch, limit=16 * MIB,
    )(weights, across, *source, u, sums, lead, own_v_x, own_v_in)
    own_v_in, part = lax.optimization_barrier((own_v_in, part))
    v_in = lax.ppermute(own_v_in, "space", pair_in)
    prev, base, lead, total = call(
        cross_kernel, [eight, eight, four, four], [VMEM] * 2 + source_specs + [VMEM] * 6,
        [scratch8] + source_scratch, limit=16 * MIB,
    )(weights, across, *source, u, first_x, coef, part, own_hi, base)
    coef_x, coef_in, prev_x, prev_in, u, send_x = call(
        far_kernel, [four, four, four, four, eight, send], [VMEM] * 11, limit=16 * MIB
    )(*source, lead, total, v_x, lead_in, sums_in, v_in, base, coef)
    gaths = []
    for n in (2, 4, 6):
        got_x, got_in = swap(send_x, u)
        part, own_hi, inner, base, gath = call(
            lambda *refs, n=n: during_kernel(n, *refs), [four, four, four, four, ((8, 2, 128), f32)],
            [VMEM] * 2 + source_specs + receiver_specs + [VMEM] * 6, [rows] + source_scratch, limit=16 * MIB,
        )(weights, across, *source, *receivers, u, prev, prev_in, coef, coef_in, got_in)
        gaths.append(gath)
        common = (weights, across, *source, u, prev, prev_x, coef, coef_x, got_x, part, own_hi, base)
        common_specs = [VMEM] * 2 + source_specs + [VMEM] * 9
        if n < 6:
            prev, prev_x, u, send_x = call(
                lambda *refs, n=n: middle_kernel(n, *refs), [eight, four, eight, send if n < 4 else ((PL,) + plane, bf16)], common_specs, [scratch8] + source_scratch, limit=16 * MIB
            )(*common)
            prev_in = inner
        else:
            final, gath = call(
                lambda *refs, n=n: last_kernel(n, *refs), [((1, PL) + plane, f32), ((8, STEPS, 128), f32)],
                [ANY, ANY] + [VMEM] * 6 + common_specs,
                [scratch8, pltpu.VMEM(*four), scratch8, scratch8, rows] + source_scratch
                + [pltpu.SMEM((1, SLOTS), jnp.int32), pltpu.SMEM((1, 1), jnp.int32), pltpu.SemaphoreType.DMA((2,)),
                   pltpu.SemaphoreType.DMA((PL,))],
                limit=20 * MIB, places=[ANY, VMEM],
            )(*receivers, *gaths, *common)
    back = lax.all_to_all(gath, "shot", split_axis=0, concat_axis=0, tiled=True)
    return final, jnp.sum(back, axis=0)[None, None]


def solution(mesh):
    placed = (
        P("shot", "space", None, None),
        P("shot", "space", None, None),
        P("shot", "space", None, None),
        P(),
        P(),
        P("shot", None),
        P("shot", None),
        P("shot", None),
        P("shot", "space", None, None),
        P("shot", "space", None, None),
        P("shot", "space"),
        P("shot", "space", None, None),
    )
    return jax.shard_map(
        on_device,
        mesh=mesh,
        in_specs=placed,
        out_specs=(P("shot", "space", None, None), P("shot", "space", None, None)),
        check_vma=False,
    )
```

```python
import jax
import jax.numpy as jnp
import numpy as np
from jax import lax
from jax.experimental import pallas as pl
from jax.experimental.pallas import tpu as pltpu
from jax.sharding import PartitionSpec as P

STEPS = 8
CAPR = 16
PL = 8
ROWS = 128
COLS = 256
EDGE = 64
SLOTS = 64
SCALE = 5040.0
TAPS = (8064.0, -1008.0, 128.0, -9.0)
CENTRE_COLS = -43008.0
CENTRE_ROWS = -42.0
COURANT = 0.09
PACK_LIMIT = 56

VMEM = pl.BlockSpec(memory_space=pltpu.VMEM)
SMEM = pl.BlockSpec(memory_space=pltpu.SMEM)
HBM = pl.BlockSpec(memory_space=pltpu.HBM)
ANY = pl.BlockSpec(memory_space=pl.ANY)
f32 = jnp.float32
bf16 = jnp.bfloat16


def band_matrix(size, centre):
    gap = np.abs(np.arange(size)[:, None] - np.arange(size)[None, :])
    out = np.where(gap == 0, centre, 0.0)
    for k in range(1, 5):
        out = np.where(gap == k, TAPS[k - 1], out)
    return out


def constants():
    cols = band_matrix(COLS, CENTRE_COLS)
    rows = band_matrix(ROWS, CENTRE_ROWS)
    return (
        jnp.asarray(np.concatenate([cols, cols], 0), bf16),
        jnp.asarray(np.concatenate([rows, rows], 1), bf16),
    )


def call(body, outs, ins, scratch=(), limit=None, cost=None, alias=None, places=None):
    return pl.pallas_call(
        body,
        out_shape=[jax.ShapeDtypeStruct(s, d) for s, d in outs],
        in_specs=ins,
        out_specs=places or [VMEM] * len(outs),
        scratch_shapes=list(scratch),
        input_output_aliases=alias or {},
        compiler_params=pltpu.CompilerParams(vmem_limit_bytes=limit),
        cost_estimate=pl.CostEstimate(flops=cost[0], bytes_accessed=cost[1], transcendentals=0) if cost else None,
    )


def is_even():
    return lax.rem(lax.axis_index("space"), 2) == 0


def mirrored4(even, plane):
    return jnp.where(even, plane, 3 - plane)


def mirrored(even, plane):
    return jnp.where(even, plane, PL - 1 - plane)


def fetch(pairs, sems):
    copies = [pltpu.make_async_copy(src, dst, sems.at[i]) for i, (src, dst) in enumerate(pairs)]
    for copy in copies:
        copy.start()
    return copies


def wait(copies):
    for copy in copies:
        copy.wait()


def pack_kernel(home_hbm, wanted_hbm, store_hbm, out_hbm, home, wanted, store, out, sems, out_sems):
    copies = fetch(((home_hbm, home), (wanted_hbm, wanted), (store_hbm, store)), sems)
    wait(copies[:2])
    me = lax.axis_index("shot")
    even = is_even()
    chosen = []
    for s in range(8):
        count = jnp.int32(0)
        slots = [jnp.int32(0), jnp.int32(0)]
        for j in range(8):
            row = home[wanted[s, j]]
            mine = lax.shift_right_logical(row, 3) == me
            for rank in range(2):
                slots[rank] = jnp.where(mine & (count == rank), row & 7, slots[rank])
            count = count + mine.astype(jnp.int32)
        chosen.append(slots)
    copies[2].wait()
    back = []
    for s in range(8):
        for q in range(PL):
            p = mirrored(even, q)
            out[s, q] = jnp.concatenate([store[chosen[s][0], p], store[chosen[s][1], p]], 1)
        copy = pltpu.make_async_copy(out.at[s], out_hbm.at[s], out_sems.at[s])
        copy.start()
        back.append(copy)
    wait(back)


def plan_kernel(home, wanted, plan):
    me = lax.axis_index("shot")
    spot = lax.broadcasted_iota(jnp.int32, (1, 128), 1)
    listed = jnp.zeros((1, 128), jnp.int32)
    homes = []
    for j in range(8):
        homes.append(lax.shift_right_logical(home[wanted[me, j]], 3))
        nth = jnp.int32(0)
        for i in range(j):
            nth = nth + (homes[i] == homes[j]).astype(jnp.int32)
        listed = jnp.where(spot == j, homes[j], jnp.where(spot == 8 + j, nth, listed))
    plan[...] = listed


def swapped(x):
    return jnp.concatenate([x[:, EDGE:], x[:, :EDGE]], 1)


def assemble_kernel(first, plan, arrived, out):
    left = lax.broadcasted_iota(jnp.int32, (EDGE, 2 * EDGE), 1) < EDGE
    owners = [plan[0, j] for j in range(8)]
    ranks = [plan[0, 8 + j] for j in range(8)]
    for j in range(0, 8, 2):
        rows = slice(j // 4 * EDGE, (j // 4 + 1) * EDGE)
        lanes = slice(j % 4 * EDGE, (j % 4 + 2) * EDGE)
        for q in range(4):
            x = arrived[owners[j], first + q]
            y = arrived[owners[j + 1], first + q]
            x = jnp.where(ranks[j] == 0, x, swapped(x))
            y = jnp.where(ranks[j + 1] == 0, swapped(y), y)
            out[q, rows, lanes] = jnp.where(left, x, y)


CHUNK = 16


def product(weights, across, u):
    hi = u.astype(bf16)
    lo = (u - hi.astype(f32)).astype(bf16)
    return jnp.dot(
        jnp.concatenate([hi, lo, across[...]], 1),
        jnp.concatenate([weights[...], hi, lo], 0),
        preferred_element_type=f32,
    )


def chunks():
    return [slice(r, r + CHUNK) for r in range(0, ROWS, CHUNK)]


def depth(get, e, low, high, r, acc):
    for k in range(1, 5):
        parts = [get(p, r) for p in (e + k, e - k) if low <= p < high]
        if parts:
            acc = acc + TAPS[k - 1] * sum(parts[1:], parts[0])
    return acc


def hat(frac):
    share = frac.astype(f32) * 0.125
    return 1.0 - share, share


def add_source(parts, even, cell, frac, pulse):
    lane = lax.broadcasted_iota(jnp.int32, (1, COLS), 1)
    wd, wr, wc = hat(frac[0, 0]), hat(frac[0, 1]), hat(frac[0, 2])
    column = jnp.where(lane == cell[0, 2], wc[0], 0.0) + jnp.where(lane == cell[0, 2] + 1, wc[1], 0.0)
    for dp in range(2):
        plane = mirrored(even, cell[0, 0] + dp - lax.axis_index("space") * PL)
        for ref, first, down in parts:
            at = first - plane if down else plane - first

            @pl.when((at >= 0) & (at < ref.shape[0]))
            def _():
                for dr in range(2):
                    row = pl.ds(cell[0, 1] + dr, 1)
                    ref[at, row, :] = ref[at, row, :] + pulse * (wd[dp] * wr[dr] * column)


GROUP = 8


def sample(fields, codes, count, spread, place, owner, rows, out):
    even = is_even()

    def group(g, _):
        for j in range(GROUP):
            r = g * GROUP + j
            code = codes[0, r]
            wr = hat(code & 7)
            wd = hat(lax.shift_right_logical(code, 3) & 7)
            y = lax.shift_right_logical(code, 6) & 127
            p = lax.shift_right_logical(code, 13)
            for f, (src, _) in enumerate(fields):
                acc = None
                for dp in range(2):
                    plane = mirrored(even, p + dp)
                    for dr in range(2):
                        term = (wd[dp] * wr[dr]) * src[plane, pl.ds(y + dr, 1), :]
                        acc = term if acc is None else acc + term
                rows[f, pl.ds(r, 1), :] = acc
        return 0

    lax.fori_loop(0, lax.div(count[0, 0] + GROUP - 1, GROUP), group, 0)
    live = lax.broadcasted_iota(jnp.int32, (SLOTS, 1), 0) < count[0, 0]
    for f, (_, n) in enumerate(fields):
        values = jnp.where(live, jnp.sum(rows[f] * spread[...], axis=1, keepdims=True), 0.0)
        placed = values * place[...]
        for q in range(8):
            out[q, n : n + 1, :] = jnp.sum(jnp.where(owner[...] == q, placed, 0.0), axis=0, keepdims=True)


def column(row):
    same = lax.broadcasted_iota(jnp.int32, (SLOTS, SLOTS), 0) == lax.broadcasted_iota(jnp.int32, (SLOTS, SLOTS), 1)
    return jnp.sum(jnp.where(same, row, 0), axis=1, keepdims=True)


def receiver_kernel(count, cells, fracs, owner, spread, place, owners, codes):
    lane = lax.broadcasted_iota(jnp.int32, (SLOTS, COLS), 1)
    share = column(fracs[2:3, :]).astype(f32) * 0.125
    at = column(cells[2:3, :])
    spread[...] = jnp.where(lane == at, 1.0 - share, 0.0) + jnp.where(lane == at + 1, share, 0.0)
    me = lax.axis_index("shot")
    slot = lax.broadcasted_iota(jnp.int32, (SLOTS, 1), 0)
    live = slot < count[0, 0]
    group = lax.broadcasted_iota(jnp.int32, (SLOTS, 128), 1)
    mine = column(owner[...])
    owners[...] = mine
    chosen = jnp.where((mine == group) & live, 1.0, 0.0)
    earlier = jnp.where(
        lax.broadcasted_iota(jnp.int32, (SLOTS, SLOTS), 1) < lax.broadcasted_iota(jnp.int32, (SLOTS, SLOTS), 0), 1.0, 0.0
    )
    before = jnp.dot(earlier.astype(bf16), chosen.astype(bf16), preferred_element_type=f32)
    rank = jnp.sum(before * chosen, axis=1, keepdims=True).astype(jnp.int32)
    place[...] = jnp.where((group == rank + me * CAPR) & live, 1.0, 0.0)
    codes[...] = ((cells[0:1, :] * ROWS + cells[1:2, :]) * 8 + fracs[0:1, :]) * 8 + fracs[1:2, :]

def open_kernel(weights, across, cur, cur_in, pri, pri_in, sums, lead, sums_in, lead_in, u, halo):
    even = is_even()
    for j in range(PL):
        u[j] = cur[0, mirrored(even, j)].astype(f32)
        halo[j] = cur_in[0, mirrored(even, j)].astype(f32)

    def now(e, r):
        return u[e, r] if e < PL else halo[e - PL, r]

    for e in range(12):
        m = product(weights, across, now(e, slice(0, ROWS)))
        for r in chunks():
            acc = depth(now, e, 0, 16, r, m[r])
            if e < PL:
                sums[e, r] = acc
                lead[e, r] = 2.0 * now(e, r) - pri[0, mirrored(even, e), r].astype(f32)
            else:
                sums_in[e - PL, r] = acc
                lead_in[e - PL, r] = 2.0 * now(e, r) - pri_in[mirrored4(even, e - PL), r].astype(f32)


def factor(x):
    scaled = x.astype(f32) * COURANT
    return scaled * scaled * (1.0 / SCALE)


def near_kernel(
    weights, across, cell_any, frac_any, pulses_any, u, sums, lead, own_v_x, plan, arrived,
    own_v_in, coef, part, own_hi, base, cell, frac, pulses, sems,
):
    source = fetch(((cell_any, cell), (frac_any, frac), (pulses_any, pulses)), sems)
    assemble_kernel(4, plan, arrived, own_v_in)
    for e in range(PL):
        for r in chunks():
            c = factor((own_v_x if e < 4 else own_v_in)[e % 4, r])
            coef[e, r] = c
            x = lead[e, r] + c * sums[e, r]
            if e < 4:
                part[e, r] = x
            else:
                own_hi[e - 4, r] = x
    wait(source)
    add_source(((own_hi, 4, False),), is_even(), cell, frac, pulses[0, 0])
    half_step(weights, across, own_hi, None, u, coef, base)


def half_step(weights, across, own_hi, inner, u, coef, base):
    for q in range(4, PL):
        m = product(weights, across, own_hi[q - 4])
        for r in chunks():
            acc = depth(lambda e, r: own_hi[e - 4, r] if e < PL else inner[e - PL, r], q, 4, 12 if inner is not None else PL, r, m[r])
            base[q - 4, r] = 2.0 * own_hi[q - 4, r] - u[q, r] + coef[q, r] * acc


def cross_kernel(
    weights, across, cell_any, frac_any, pulses_any, u, got_x, coef, part, own_hi, base_hi,
    own, base, outer_lead, outer_sum, halo, cell, frac, pulses, sems,
):
    source = fetch(((cell_any, cell), (frac_any, frac), (pulses_any, pulses)), sems)
    even = is_even()
    for j in range(PL):
        halo[j] = got_x[mirrored(even, PL - 1 - j)].astype(f32)

    def now(e, r):
        return halo[-1 - e, r] if e < 0 else u[e, r]

    for q in range(4):
        for r in chunks():
            own[q, r] = part[q, r] + coef[q, r] * depth(now, q, -8, 0, r, 0.0)
            own[q + 4, r] = own_hi[q, r]
    for e in range(-4, 0):
        j = -1 - e
        m = product(weights, across, halo[j])
        for r in chunks():
            outer_sum[j, r] = depth(now, e, -8, PL, r, m[r])
            outer_lead[j, r] = 2.0 * halo[j, r] - got_x[PL + mirrored4(even, 3 - j), r].astype(f32)
    wait(source)
    add_source(((own.at[pl.ds(0, 4)], 0, False),), even, cell, frac, pulses[0, 0])

    def following(e, r):
        return own[e, r]

    for q in range(4):
        m = product(weights, across, own[q])
        for r in chunks():
            acc = depth(following, q, 0, PL, r, m[r])
            base[q, r] = 2.0 * own[q, r] - u[q, r] + coef[q, r] * acc
    for q in range(4, PL):
        for r in chunks():
            base[q, r] = base_hi[q - 4, r] + coef[q, r] * depth(following, q, 0, 4, r, 0.0)


def bundle_kernel(cur, pri, both, half, sems):
    first = jnp.where(is_even(), 0, 4)
    wait(
        fetch(
            (
                (cur.at[0], both.at[pl.ds(0, PL)]),
                (pri.at[0, pl.ds(first, 4)], both.at[pl.ds(PL, 4)]),
                (pri.at[0, pl.ds(4 - first, 4)], half),
            ),
            sems,
        )
    )


def pack_send(u, out):
    for q in range(PL):
        out[q] = u[q].astype(bf16)
    if out.shape[0] > PL:
        edge = u[0]
        out[PL] = (edge - edge.astype(bf16).astype(f32)).astype(bf16)


def far_kernel(
    cell, frac, pulses, lead_x, sums_x, v_x, lead_in, sums_in, v_in, base, coef,
    coef_x, coef_in, outer, inner, last, send_x,
):
    even = is_even()
    for j in range(4):
        for r in chunks():
            c = factor(v_x[j, r])
            coef_x[j, r] = c
            outer[j, r] = lead_x[j, r] + c * sums_x[j, r]
            c = factor(v_in[3 - j, r])
            coef_in[j, r] = c
            inner[j, r] = lead_in[j, r] + c * sums_in[j, r]
    add_source(((outer, -1, True), (inner, PL, False)), even, cell, frac, pulses[0, 0])
    for q in range(PL):
        for r in chunks():
            if q < 4:
                acc = depth(lambda e, r: outer[-1 - e, r], q, -4, 0, r, 0.0)
            else:
                acc = depth(lambda e, r: inner[e - PL, r], q, PL, 12, r, 0.0)
            last[q, r] = base[q, r] + coef[q, r] * acc
    add_source(((last, 0, False),), even, cell, frac, pulses[0, 1])
    pack_send(last, send_x)


def during_kernel(
    step, weights, across, cell_any, frac_any, pulses_any, codes, count, owner, spread, place, u, prev, prev_in, coef, coef_in, got_in,
    part, own_hi, inner, base, gath, rows, cell, frac, pulses, sems,
):
    source = fetch(((cell_any, cell), (frac_any, frac), (pulses_any, pulses)), sems)
    even = is_even()
    def now(e, r):
        return u[e, r] if e < PL else got_in[2 * PL - 1 - e, r]

    whole = slice(0, ROWS)
    for e in range(12):
        m = product(weights, across, now(e, whole))
        for r in chunks():
            acc = depth(now, e, 0, 16, r, m[r])
            if e < PL:
                x = 2.0 * u[e, r] - prev[e, r] + coef[e, r] * acc
                if e < 4:
                    part[e, r] = x
                else:
                    own_hi[e - 4, r] = x
            else:
                inner[e - PL, r] = 2.0 * now(e, r) - prev_in[e - PL, r] + coef_in[e - PL, r] * acc
    wait(source)
    add_source(((own_hi, 4, False), (inner, PL, False)), even, cell, frac, pulses[0, step])
    half_step(weights, across, own_hi, inner, u, coef, base)
    sample(((prev, 0), (u, 1)), codes, count, spread, place, owner, rows, gath)


def after_kernel(
    step, weights, across, source, u, prev, prev_x, coef, coef_x, got_x, part, own_hi, base,
    own, outer, last, halo,
):
    copies, cell, frac, pulses = source
    even = is_even()
    for j in range(PL):
        x = got_x[j].astype(f32)
        halo[j] = x + got_x[PL].astype(f32) if j == 0 and got_x.shape[0] > PL else x

    def now(e, r):
        return halo[-1 - e, r] if e < 0 else u[e, r]

    whole = slice(0, ROWS)
    for e in range(-4, 0):
        j = -1 - e
        m = product(weights, across, halo[j])
        for r in chunks():
            acc = depth(now, e, -8, 8, r, m[r])
            outer[j, r] = 2.0 * halo[j, r] - prev_x[j, r] + coef_x[j, r] * acc
    for q in range(4):
        for r in chunks():
            own[q, r] = part[q, r] + coef[q, r] * depth(now, q, -8, 0, r, 0.0)
            own[q + 4, r] = own_hi[q, r]
    wait(copies)
    add_source(((outer, -1, True), (own.at[pl.ds(0, 4)], 0, False)), even, cell, frac, pulses[0, step])

    def following(e, r):
        return outer[-1 - e, r] if e < 0 else own[e, r]

    for q in range(4):
        m = product(weights, across, own[q])
        for r in chunks():
            acc = depth(following, q, -4, 8, r, m[r])
            last[q, r] = 2.0 * own[q, r] - u[q, r] + coef[q, r] * acc
    for q in range(4, PL):
        for r in chunks():
            last[q, r] = base[q - 4, r] + coef[q, r] * depth(following, q, 0, 4, r, 0.0)


def middle_kernel(step, weights, across, cell_any, frac_any, pulses_any, *refs):
    own, outer, last, send_x, halo, cell, frac, pulses, sems = refs[-9:]
    copies = fetch(((cell_any, cell), (frac_any, frac), (pulses_any, pulses)), sems)
    source = (copies, cell, frac, pulses)
    after_kernel(step, weights, across, source, *refs[:-9], own, outer, last, halo)
    add_source(((last, 0, False),), is_even(), cell, frac, pulses[0, step + 1])
    pack_send(last, send_x)


def gather_kernel(back, out):
    total = back[0]
    for s in range(1, 8):
        total = total + back[s]
    out[0, 0] = total


def last_kernel(
    step, codes_any, count_any, owner, spread, place, gath_a, gath_b, gath_c,
    weights, across, cell_any, frac_any, pulses_any, *refs,
):
    final, gath, own, outer, last, halo, rows, cell, frac, pulses, sems, codes, count, more_sems, final_sems = refs[-15:]
    copies = fetch(((cell_any, cell), (frac_any, frac), (pulses_any, pulses)), sems)
    more = fetch(((codes_any, codes), (count_any, count)), more_sems)
    even = is_even()
    source = (copies, cell, frac, pulses)
    after_kernel(step, weights, across, source, *refs[:-15], own, outer, last, halo)
    add_source(((last, 0, False),), even, cell, frac, pulses[0, step + 1])
    back = fetch([(last.at[q], final.at[0, mirrored(even, q)]) for q in range(PL)], final_sems)
    for i, some in enumerate((gath_a, gath_b, gath_c)):
        gath[:, 2 * i : 2 * i + 2, :] = some[...]
    wait(more)
    sample(((own, step), (last, step + 1)), codes, count, spread, place, owner, rows, gath)
    wait(back)


MIB = 1 << 20


def on_device(
    prior_field, current_field, model_store, tile_home, aperture, source_cell, source_frac,
    wavelet, receiver_cell, receiver_frac, receiver_count, trace_owner,
):
    size = lax.axis_size("space")
    pair_in = [(i, i ^ 1) for i in range(size)]
    pair_x = [(i, i + 1) for i in range(1, size - 1, 2)] + [(i + 1, i) for i in range(1, size - 1, 2)]

    def swap(across_chips, in_chip):
        return lax.ppermute(across_chips, "space", pair_x), lax.ppermute(in_chip, "space", pair_in)

    weights, across = constants()
    plane = (ROWS, COLS)
    four = ((4,) + plane, f32)
    eight = ((PL,) + plane, f32)
    tile_planes = ((4,) + plane, bf16)
    send = ((PL + 1,) + plane, bf16)
    scratch8 = pltpu.VMEM(*eight)
    rows = pltpu.VMEM((2, SLOTS, COLS), f32)

    out = call(
        pack_kernel, [((8, PL, EDGE, 2 * EDGE), bf16)], [HBM] * 3,
        [pltpu.SMEM((64,), jnp.int32), pltpu.SMEM((8, 8), jnp.int32), pltpu.VMEM((8, PL, EDGE, EDGE), bf16),
         pltpu.VMEM((8, PL, EDGE, 2 * EDGE), bf16), pltpu.SemaphoreType.DMA((3,)), pltpu.SemaphoreType.DMA((8,))],
        limit=PACK_LIMIT * MIB, places=[HBM],
    )(tile_home, aperture, model_store)[0]
    plan = call(plan_kernel, [((1, 128), jnp.int32)], [SMEM, SMEM], limit=4 * MIB)(tile_home, aperture)[0]
    arrived = lax.all_to_all(out, "shot", split_axis=0, concat_axis=0, tiled=True)
    both, half = call(
        bundle_kernel, [((12,) + plane, bf16), tile_planes], [ANY, ANY], [pltpu.SemaphoreType.DMA((3,))],
        limit=4 * MIB, places=[ANY, ANY],
    )(current_field, prior_field)
    first_x, pri_in = swap(both, half)
    cur_in = lax.ppermute(current_field, "space", pair_in)
    spread, place, owners, codes = call(
        receiver_kernel,
        [((SLOTS, COLS), f32), ((SLOTS, 128), f32), ((SLOTS, 1), jnp.int32), ((1, SLOTS), jnp.int32)],
        [SMEM] + [VMEM] * 3, limit=4 * MIB,
    )(
        receiver_count, jnp.transpose(receiver_cell[0, 0]), jnp.transpose(receiver_frac[0, 0]),
        jnp.transpose(trace_owner[0, 0]),
    )
    sums, lead, sums_in, lead_in, u = call(
        open_kernel, [eight, eight, four, four, eight], [VMEM] * 6, [scratch8], limit=16 * MIB
    )(weights, across, current_field, cur_in, prior_field, pri_in)
    arrived, sums, lead, u = lax.optimization_barrier((arrived, sums, lead, u))
    own_v_x = call(lambda *refs: assemble_kernel(0, *refs), [tile_planes], [VMEM, VMEM], limit=8 * MIB)(plan, arrived)[0]
    v_x = lax.ppermute(own_v_x, "space", pair_x)
    source = (source_cell, source_frac, wavelet)
    source_specs = [ANY] * 3
    source_scratch = [
        pltpu.SMEM((1, 3), jnp.int32), pltpu.SMEM((1, 3), jnp.int32), pltpu.SMEM((1, STEPS), f32), pltpu.SemaphoreType.DMA((3,)),
    ]
    receivers = (codes, receiver_count, owners, spread, place)
    receiver_specs = [SMEM, SMEM, VMEM, VMEM, VMEM]
    own_v_in, coef, part, own_hi, base = call(
        near_kernel, [tile_planes, eight, four, four, four], [VMEM] * 2 + source_specs + [VMEM] * 6,
        source_scratch, limit=16 * MIB,
    )(weights, across, *source, u, sums, lead, own_v_x, plan, arrived)
    v_in = lax.ppermute(own_v_in, "space", pair_in)
    prev, base, lead, total = call(
        cross_kernel, [eight, eight, four, four], [VMEM] * 2 + source_specs + [VMEM] * 6,
        [scratch8] + source_scratch, limit=16 * MIB,
    )(weights, across, *source, u, first_x, coef, part, own_hi, base)
    coef_x, coef_in, prev_x, prev_in, u, send_x = call(
        far_kernel, [four, four, four, four, eight, send], [VMEM] * 11, limit=16 * MIB
    )(*source, lead, total, v_x, lead_in, sums_in, v_in, base, coef)
    gaths = []
    for n in (2, 4, 6):
        got_x, got_in = swap(send_x, u)
        part, own_hi, inner, base, gath = call(
            lambda *refs, n=n: during_kernel(n, *refs), [four, four, four, four, ((8, 2, 128), f32)],
            [VMEM] * 2 + source_specs + receiver_specs + [VMEM] * 6, [rows] + source_scratch, limit=16 * MIB,
        )(weights, across, *source, *receivers, u, prev, prev_in, coef, coef_in, got_in)
        gaths.append(gath)
        common = (weights, across, *source, u, prev, prev_x, coef, coef_x, got_x, part, own_hi, base)
        common_specs = [VMEM] * 2 + source_specs + [VMEM] * 9
        if n < 6:
            prev, prev_x, u, send_x = call(
                lambda *refs, n=n: middle_kernel(n, *refs), [eight, four, eight, send if n < 4 else ((PL,) + plane, bf16)], common_specs, [scratch8] + source_scratch, limit=16 * MIB
            )(*common)
            prev_in = inner
        else:
            final, gath = call(
                lambda *refs, n=n: last_kernel(n, *refs), [((1, PL) + plane, f32), ((8, STEPS, 128), f32)],
                [ANY, ANY] + [VMEM] * 6 + common_specs,
                [scratch8, pltpu.VMEM(*four), scratch8, scratch8, rows] + source_scratch
                + [pltpu.SMEM((1, SLOTS), jnp.int32), pltpu.SMEM((1, 1), jnp.int32), pltpu.SemaphoreType.DMA((2,)),
                   pltpu.SemaphoreType.DMA((PL,))],
                limit=20 * MIB, places=[ANY, VMEM],
            )(*receivers, *gaths, *common)
    back = lax.all_to_all(gath, "shot", split_axis=0, concat_axis=0, tiled=True)
    gathers = call(gather_kernel, [((1, 1, STEPS, 128), f32)], [VMEM], limit=4 * MIB)(back)[0]
    return final, gathers


def solution(mesh):
    placed = (
        P("shot", "space", None, None),
        P("shot", "space", None, None),
        P("shot", "space", None, None),
        P(),
        P(),
        P("shot", None),
        P("shot", None),
        P("shot", None),
        P("shot", "space", None, None),
        P("shot", "space", None, None),
        P("shot", "space"),
        P("shot", "space", None, None),
    )
    return jax.shard_map(
        on_device,
        mesh=mesh,
        in_specs=placed,
        out_specs=(P("shot", "space", None, None), P("shot", "space", None, None)),
        check_vma=False,
    )
```
